32 devices in a mesh: grp: 2 (over x), seq: 4 (over z), frm: 4 (over y, core).
Axes of the slice: x: 2, y: 2, z: 4, core: 2. Of those that a mesh axis runs over, the one named last changes fastest.
Arguments:
- residual: bfloat16 [8, 512, 1152], P(('grp', 'frm'), 'seq'), parts along dimension 0, may hold values from -6 to 6
- spatial_query: bfloat16 [8, 512, 1152], P(('grp', 'frm'), 'seq'), parts along dimension 0, may hold values from -6 to 6
- spatial_key: bfloat16 [8, 512, 1152], P(('grp', 'frm'), 'seq'), parts along dimension 0, may hold values from -6 to 6
- spatial_value: bfloat16 [8, 512, 1152], P(('grp', 'frm'), 'seq'), parts along dimension 0, may hold values from -6 to 6
- out_weight: bfloat16 [1152, 1152], replicated, may hold values from -0.1875 to 0.1875
- qkv_weight: bfloat16 [3, 1152, 1152], replicated, may hold values from -0.1875 to 0.1875
- space_gains: float32 [2, 72], replicated, may hold values from 1 to 2
- time_gains: float32 [2, 72], replicated, may hold values from 1 to 2
- cotangent: bfloat16 [8, 512, 1152], P(('grp', 'frm'), 'seq'), parts along dimension 0, may hold values from -6 to 6
Outputs:
- grad_residual: bfloat16 [8, 512, 1152], P(('grp', 'frm'), 'seq'), parts along dimension 0
- grad_query: bfloat16 [8, 512, 1152], P(('grp', 'frm'), 'seq'), parts along dimension 0
- grad_key: bfloat16 [8, 512, 1152], P(('grp', 'frm'), 'seq'), parts along dimension 0
- grad_value: bfloat16 [8, 512, 1152], P(('grp', 'frm'), 'seq'), parts along dimension 0
The draws below stay inside these ranges and needn't reach their ends.
There are 2 independent parts, one for each index of `grp`. The reference program is written for one: setup_inputs(seed, part) draws one part's arguments, and reference() takes and returns one part's arrays. A program takes and returns all parts, laid end to end along the dimension named above; an argument that names none is the same for every part. Nothing has to cross between parts.
All inputs are finite; a program needn't handle non-finite values.
Results may differ from the reference program's by a relative error of at most 0.033.
Values may be sent and summed in bfloat16 or wider, within the bound.
No kernel may reach another device: no remote copies, remote signals or barrier semaphores. Data moves between devices by JAX's collectives and lax.ppermute only.
A program may use at most 128 MiB of HBM per device.

```python
import jax
import jax.numpy as jnp
from jax import lax

HD = 72
D = 1152
S = 512
F = 4


def level_of(stream_key, dims, cuts, low, largest):
    level, own = 1.0, jax.random.fold_in(stream_key, 6)
    for axis_at, shards_of in cuts:
        draws = jnp.exp(jax.random.uniform(jax.random.fold_in(own, axis_at), (shards_of,), jnp.float32, low / len(cuts), largest / len(cuts)))
        level = level * jnp.repeat(draws, dims[axis_at] // shards_of).reshape([-1 if axis == axis_at else 1 for axis in range(len(dims))])
    return level


def noise(own_key, dims, scale, most, split=(), held_as=jnp.bfloat16):
    array = jax.random.normal(own_key, dims, jnp.float32) * scale
    if len(split) > 0:
        array = level_of(own_key, dims, split, -0.22, 0.18) * array
    return jnp.clip(array, min=-most, max=most).astype(held_as)


def setup_inputs(seed: int = 0, part: int = 0) -> dict:
    key_of = jax.random.split(jax.random.key(seed), 10)
    part_keys = jax.random.split(jax.random.fold_in(key_of[9], part), 10)
    return {
        "residual": noise(part_keys[0], (F, S, D), 1.0, 6.0, ((0, 4), (1, 4))),
        "spatial_query": noise(part_keys[1], (F, S, D), 1.0, 6.0, ((0, 4), (1, 4))),
        "spatial_key": noise(part_keys[2], (F, S, D), 1.0, 6.0, ((0, 4), (1, 4))),
        "spatial_value": noise(part_keys[3], (F, S, D), 1.0, 6.0, ((0, 4), (1, 4))),
        "out_weight": noise(key_of[4], (D, D), D ** -0.5, 0.1875),
        "qkv_weight": noise(key_of[5], (3, D, D), D ** -0.5, 0.1875),
        "space_gains": jnp.clip(jax.random.uniform(key_of[6], (2, HD), jnp.float32, 1.0, 2.0), 1.0, 2.0),
        "time_gains": jnp.clip(jax.random.uniform(key_of[7], (2, HD), jnp.float32, 1.0, 2.0), 1.0, 2.0),
        "cotangent": noise(part_keys[8], (F, S, D), 1.0, 6.0, ((0, 4), (1, 4))),
    }


norm_eps = 1e-06
space_forms = ('blhd,bmhd->bhlm', 'bhlm,bmhd->blhd', 'bhlm,blhd->bmhd')
time_forms = ('lbhd,mbhd->bhlm', 'bhlm,mbhd->lbhd', 'bhlm,lbhd->mbhd')

def product(form, left, right):
    return jnp.einsum(form, left.astype(jnp.float32), right.astype(jnp.float32))

def head_norm(tensor):
    widened = tensor.astype(jnp.float32)
    inverse = lax.rsqrt(lax.optimization_barrier(jnp.mean(widened * widened, axis=-1, keepdims=True)) + norm_eps)
    return (widened * inverse, inverse)

def norm_back(upward, normed, inverse, gain):
    scaled = upward * gain
    return inverse * (scaled - normed * lax.optimization_barrier(jnp.mean(scaled * normed, axis=-1, keepdims=True)))

def attend_fwd(query_in, key_in, value_in, gain_pair, form_set):
    query_hat, query_inv = head_norm(query_in)
    key_hat, key_inv = head_norm(key_in)
    query_nrm = (query_hat * gain_pair[0]).astype(jnp.bfloat16)
    key_nrm = (key_hat * gain_pair[1]).astype(jnp.bfloat16)
    factor = query_in.shape[-1] ** (-0.5)
    scores = product(form_set[0], query_nrm, key_nrm) * factor
    expons = jnp.exp(scores)
    shares = expons / lax.optimization_barrier(jnp.sum(expons, axis=-1, keepdims=True))
    weights = shares.astype(jnp.bfloat16)
    output = product(form_set[1], weights, value_in).astype(jnp.bfloat16)
    stored = (query_hat, key_hat, query_inv, key_inv, query_nrm, key_nrm, shares, weights)
    return (output, stored)

def attend_bwd(stored, upward, value_in, gain_pair, form_set):
    query_hat, key_hat, query_inv, key_inv, query_nrm, key_nrm, shares, weights = stored
    factor = query_hat.shape[-1] ** (-0.5)
    share_grad = product(form_set[0], upward, value_in)
    centre = lax.optimization_barrier(jnp.sum(shares * share_grad, axis=-1, keepdims=True))
    score_grad = (shares * (share_grad - centre) * factor).astype(jnp.bfloat16)
    query_grad = product(form_set[1], score_grad, key_nrm)
    key_grad = product(form_set[2], score_grad, query_nrm)
    value_grad = product(form_set[2], weights, upward).astype(jnp.bfloat16)
    return (norm_back(query_grad, query_hat, query_inv, gain_pair[0]).astype(jnp.bfloat16), norm_back(key_grad, key_hat, key_inv, gain_pair[1]).astype(jnp.bfloat16), value_grad)

def layer_norm(tokens_in):
    widened = tokens_in.astype(jnp.float32)
    centred = widened - lax.optimization_barrier(jnp.mean(widened, axis=-1, keepdims=True))
    inverse = lax.rsqrt(lax.optimization_barrier(jnp.mean(centred * centred, axis=-1, keepdims=True)) + norm_eps)
    return (centred * inverse, inverse)

def layer_back(upward, normed, inverse):
    return inverse * (upward - lax.optimization_barrier(jnp.mean(upward, axis=-1, keepdims=True)) - normed * lax.optimization_barrier(jnp.mean(upward * normed, axis=-1, keepdims=True)))

def split_heads(tensor):
    return tensor.reshape(tensor.shape[:-1] + (tensor.shape[-1] // HD, HD))

def merge_heads(tensor):
    return tensor.reshape(tensor.shape[:-2] + (tensor.shape[-2] * tensor.shape[-1],))

def reference(residual, spatial_query, spatial_key, spatial_value, out_weight, qkv_weight, space_gains, time_gains, cotangent):

    def space_forward(triple):
        output, stored = attend_fwd(triple[0][None], triple[1][None], triple[2][None], space_gains, space_forms)
        return output[0]
    split_query = split_heads(spatial_query)
    split_key = split_heads(spatial_key)
    split_value = split_heads(spatial_value)
    attended = lax.map(space_forward, (split_query, split_key, split_value))
    mixed = (residual.astype(jnp.float32) + jnp.dot(merge_heads(attended), out_weight, preferred_element_type=jnp.float32)).astype(jnp.bfloat16)
    normed, inverse = layer_norm(mixed)
    lowered = normed.astype(jnp.bfloat16)
    query_t = jnp.dot(lowered, qkv_weight[0], preferred_element_type=jnp.float32).astype(jnp.bfloat16)
    key_t = jnp.dot(lowered, qkv_weight[1], preferred_element_type=jnp.float32).astype(jnp.bfloat16)
    value_t = jnp.dot(lowered, qkv_weight[2], preferred_element_type=jnp.float32).astype(jnp.bfloat16)
    temporal_out, stored = attend_fwd(split_heads(query_t), split_heads(key_t), split_heads(value_t), time_gains, time_forms)
    grads = attend_bwd(stored, split_heads(cotangent), split_heads(value_t), time_gains, time_forms)
    upward = jnp.dot(merge_heads(grads[0]), qkv_weight[0].T, preferred_element_type=jnp.float32)
    upward = upward + jnp.dot(merge_heads(grads[1]), qkv_weight[1].T, preferred_element_type=jnp.float32)
    upward = upward + jnp.dot(merge_heads(grads[2]), qkv_weight[2].T, preferred_element_type=jnp.float32)
    grad_residual = layer_back(upward, normed, inverse).astype(jnp.bfloat16)
    space_up = jnp.dot(grad_residual, out_weight.T, preferred_element_type=jnp.float32).astype(jnp.bfloat16)

    def space_backward(quartet):
        output, kept = attend_fwd(quartet[0][None], quartet[1][None], quartet[2][None], space_gains, space_forms)
        result = attend_bwd(kept, quartet[3][None], quartet[2][None], space_gains, space_forms)
        return (result[0][0], result[1][0], result[2][0])
    triple = lax.map(space_backward, (split_query, split_key, split_value, split_heads(space_up)))
    return (grad_residual, merge_heads(triple[0]), merge_heads(triple[1]), merge_heads(triple[2]))
```

```python
import functools

import jax
import jax.numpy as jnp
from jax import lax
from jax.experimental import pallas as pl
from jax.experimental.pallas import tpu as pltpu
from jax.sharding import PartitionSpec as P

HD = 72
EPS = 1e-06
F32 = jnp.float32
BF16 = jnp.bfloat16
LANES = 128
VMEM_LIMIT = 56 * 1024 * 1024

PARAMS = pltpu.CompilerParams(vmem_limit_bytes=VMEM_LIMIT)


def dot(left, right, dims):
    return lax.dot_general(left, right, (dims, ((), ())), preferred_element_type=F32)


def rounded(value):
    return value.astype(BF16).astype(F32)


def head_norm(tensor):
    inverse = lax.rsqrt(jnp.mean(tensor * tensor, axis=-2, keepdims=True) + EPS)
    return (tensor * inverse, inverse)


def norm_back(upward, hat, inverse, gain):
    scaled = upward * gain
    return inverse * (scaled - hat * jnp.mean(scaled * hat, axis=-2, keepdims=True))


def exchange_lanes(blocks, width):
    count = len(blocks)
    group = lax.broadcasted_iota(jnp.int32, blocks[0].shape, 1) // width
    results = []
    for a in range(count):
        result = None
        for b in range(count):
            shift = (width * (b - a)) % (width * count)
            moved = blocks[b] if shift == 0 else pltpu.roll(blocks[b], shift, 1)
            result = moved if result is None else jnp.where(group == b, moved, result)
        results.append(result)
    return results


def is_dense(rows, parts):
    return rows % (8 * parts) == 0


def pack(tile, parts):
    rows, width = tile.shape[0], tile.shape[1] // parts
    if is_dense(rows, parts):
        own = rows // parts
        return exchange_lanes([tile[b * own : (b + 1) * own] for b in range(parts)], width)
    return [tile[:, b * width : (b + 1) * width] for b in range(parts)]


def unpack(blocks):
    parts = len(blocks)
    if blocks[0].shape[1] * parts == LANES:
        return jnp.concatenate(blocks, axis=1)
    return jnp.concatenate(exchange_lanes(blocks, blocks[0].shape[1] // parts), axis=0)


def block_shape(rows, parts):
    if is_dense(rows, parts):
        return (rows // parts, LANES)
    return (rows, LANES // parts)


def turn_kernel(axis, q_ref, k_ref, v_ref, *rest):
    out_refs, held = rest[:-1], rest[-1]
    count = len(out_refs)
    rows = out_refs[0].shape[1]
    me = lax.axis_index(axis)
    for n, ref in enumerate((q_ref, k_ref, v_ref)):
        held[n] = ref[...].astype(F32).T.astype(BF16)
    for s in range(count):
        start = pl.multiple_of((me ^ s) * rows, rows)
        out_refs[s][...] = held[:, pl.ds(start, rows), :]


def turn(axis, count, arrays):
    tokens, width = arrays[0].shape
    return pl.pallas_call(
        functools.partial(turn_kernel, axis),
        out_shape=[jax.ShapeDtypeStruct((3, width // count, tokens), BF16)] * count,
        scratch_shapes=[pltpu.VMEM((3, width, tokens), BF16)],
        compiler_params=PARAMS,
        name="turn",
    )(*arrays)


def unturn_kernel(axis, *refs):
    count = len(refs) - 4
    in_refs, out_refs, held = refs[:count], refs[count:-1], refs[-1]
    rows = in_refs[0].shape[1]
    me = lax.axis_index(axis)
    for s in range(count):
        start = pl.multiple_of((me ^ s) * rows, rows)
        held[:, pl.ds(start, rows), :] = in_refs[s][...]
    for n, ref in enumerate(out_refs):
        ref[...] = held[n].astype(F32).T.astype(BF16)


def unturn(axis, arrays):
    count = len(arrays)
    _, rows, tokens = arrays[0].shape
    return pl.pallas_call(
        functools.partial(unturn_kernel, axis),
        out_shape=[jax.ShapeDtypeStruct((tokens, rows * count), BF16)] * 3,
        scratch_shapes=[pltpu.VMEM((3, rows * count, tokens), BF16)],
        compiler_params=PARAMS,
        name="unturn",
    )(*arrays)


def gather_part(refs, part):
    return jnp.concatenate([ref[part].astype(F32) for ref in refs], axis=1)


def space_fwd_kernel(axis, parts, gain_ref, *refs):
    in_refs, out_ref, held = refs[:-2], refs[-2], refs[-1]
    count = len(in_refs)
    rows = in_refs[0].shape[1]
    me = lax.axis_index(axis)
    query, key, value = (gather_part(in_refs, n) for n in range(3))
    factor = HD ** (-0.5)
    for h in range(rows // HD):
        cut = slice(h * HD, (h + 1) * HD)
        query_nrm = (head_norm(query[cut])[0] * gain_ref[0]).astype(BF16)
        key_nrm = (head_norm(key[cut])[0] * gain_ref[1]).astype(BF16)
        scores = dot(key_nrm, query_nrm, ((0,), (0,)))
        expons = jnp.exp(scores * factor)
        total = jnp.sum(expons, axis=0, keepdims=True)
        attended = dot(value[cut].astype(BF16), expons.astype(BF16), ((1,), (0,)))
        held[cut, :] = attended * (1.0 / total)
    for s in range(count):
        blocks = pack(held[:, s * LANES : (s + 1) * LANES], parts)
        for f, block in enumerate(blocks):
            out_ref[(me ^ s) * parts + f] = block.astype(BF16)


def space_fwd(axis, parts, gains, arrays):
    count = len(arrays)
    _, rows, tokens = arrays[0].shape
    return pl.pallas_call(
        functools.partial(space_fwd_kernel, axis, parts),
        out_shape=jax.ShapeDtypeStruct((count * parts,) + block_shape(rows, parts), BF16),
        scratch_shapes=[pltpu.VMEM((rows, count * tokens), F32)],
        compiler_params=PARAMS,
        name="space_fwd",
    )(gains, *arrays)


def space_bwd_kernel(axis, parts, gain_ref, up_ref, *refs):
    count = (len(refs) - 1) // 2
    in_refs, out_refs, held = refs[:count], refs[count:-1], refs[-1]
    rows = in_refs[0].shape[1]
    me = lax.axis_index(axis)
    for s in range(count):
        blocks = [up_ref[(me ^ s) * parts + f].astype(F32) for f in range(parts)]
        held[:, s * LANES : (s + 1) * LANES] = unpack(blocks)
    query, key, value = (gather_part(in_refs, n) for n in range(3))
    factor = HD ** (-0.5)
    grads = []
    for h in range(rows // HD):
        cut = slice(h * HD, (h + 1) * HD)
        query_hat, query_inv = head_norm(query[cut])
        key_hat, key_inv = head_norm(key[cut])
        query_nrm = (query_hat * gain_ref[0]).astype(BF16)
        key_nrm = (key_hat * gain_ref[1]).astype(BF16)
        up = held[cut, :].astype(BF16)
        scores = dot(key_nrm, query_nrm, ((0,), (0,)))
        expons = jnp.exp(scores * factor)
        shares = expons * (1.0 / jnp.sum(expons, axis=0, keepdims=True))
        share_grad = dot(value[cut].astype(BF16), up, ((0,), (0,)))
        centre = jnp.sum(shares * share_grad, axis=0, keepdims=True)
        score_grad = (shares * (share_grad - centre) * factor).astype(BF16)
        query_grad = dot(key_nrm, score_grad, ((1,), (0,)))
        key_grad = dot(query_nrm, score_grad, ((1,), (1,)))
        value_grad = dot(up, shares.astype(BF16), ((1,), (1,)))
        grads.append(
            (
                norm_back(query_grad, query_hat, query_inv, gain_ref[0]),
                norm_back(key_grad, key_hat, key_inv, gain_ref[1]),
                value_grad,
            )
        )
    for n in range(3):
        whole = jnp.concatenate([grad[n] for grad in grads], axis=0).astype(BF16)
        for s in range(count):
            out_refs[s][n] = whole[:, s * LANES : (s + 1) * LANES]


def space_bwd(axis, parts, gains, up, arrays):
    count = len(arrays)
    _, rows, tokens = arrays[0].shape
    return pl.pallas_call(
        functools.partial(space_bwd_kernel, axis, parts),
        out_shape=[jax.ShapeDtypeStruct((3, rows, tokens), BF16)] * count,
        scratch_shapes=[pltpu.VMEM((rows, count * tokens), F32)],
        compiler_params=PARAMS,
        name="space_bwd",
    )(gains, up, *arrays)


def time_head(query_in, key_in, value, upward, query_gain, key_gain, parts):
    width = LANES // parts
    factor = HD ** (-0.5)
    query_hat, query_inv = head_norm(query_in)
    key_hat, key_inv = head_norm(key_in)
    query_nrm = rounded(query_hat * query_gain)
    key_nrm = rounded(key_hat * key_gain)

    def turned(tensor, r):
        shift = (r * width) % LANES
        return tensor if shift == 0 else pltpu.roll(tensor, shift, 1)

    keys = [turned(key_nrm, r) for r in range(parts)]
    expons = [jnp.exp(jnp.sum(query_nrm * keys[r], axis=0, keepdims=True) * factor) for r in range(parts)]
    scale = 1.0 / functools.reduce(jnp.add, expons)
    shares = [expon * scale for expon in expons]
    share_grads = [jnp.sum(upward * turned(value, r), axis=0, keepdims=True) for r in range(parts)]
    centre = functools.reduce(jnp.add, [a * b for a, b in zip(shares, share_grads)])
    score_grads = [rounded(shares[r] * (share_grads[r] - centre) * factor) for r in range(parts)]
    query_grad = functools.reduce(jnp.add, [score_grads[r] * keys[r] for r in range(parts)])
    key_grad = functools.reduce(jnp.add, [turned(score_grads[r] * query_nrm, -r) for r in range(parts)])
    value_grad = functools.reduce(jnp.add, [turned(rounded(shares[r]) * upward, -r) for r in range(parts)])
    return (
        norm_back(query_grad, query_hat, query_inv, query_gain),
        norm_back(key_grad, key_hat, key_inv, key_gain),
        value_grad,
    )


def middle_kernel(
    count,
    parts,
    att_ref,
    res_ref,
    cot_ref,
    gain_ref,
    ow_hbm,
    qw_hbm,
    gr_ref,
    up_ref,
    ow_ref,
    qw_ref,
    att_s,
    low_s,
    cot_s,
    qkv_s,
    grad_s,
    sems,
):
    width = ow_ref.shape[0]
    rows = width // count
    copies = [pltpu.make_async_copy(ow_hbm, ow_ref, sems.at[0])]
    copies += [pltpu.make_async_copy(qw_hbm.at[n], qw_ref.at[n], sems.at[1 + n]) for n in range(3)]
    for copy in copies:
        copy.start()
    for z in range(count):
        att_s[z * rows : (z + 1) * rows, :] = unpack(
            [att_ref[z * parts + f].astype(F32) for f in range(parts)]
        )
    attended = att_s[...].T.astype(BF16)
    cot_s[...] = cot_ref[...].reshape(LANES, width).astype(F32).T
    copies[0].wait()
    mixed = rounded(
        res_ref[...].reshape(LANES, width).astype(F32) + dot(attended, ow_ref[...], ((1,), (0,)))
    )
    centred = mixed - jnp.mean(mixed, axis=1, keepdims=True)
    inverse = lax.rsqrt(jnp.mean(centred * centred, axis=1, keepdims=True) + EPS)
    normed = centred * inverse
    low_s[...] = normed
    lowered = normed.astype(BF16)
    for n in range(3):
        copies[1 + n].wait()
        product = rounded(dot(lowered, qw_ref[n], ((1,), (0,))))
        qkv_s[n] = product.T
    for h in range(width // HD):
        cut = slice(h * HD, (h + 1) * HD)
        grads = time_head(
            qkv_s[0, cut], qkv_s[1, cut], qkv_s[2, cut], cot_s[cut], gain_ref[0], gain_ref[1], parts
        )
        for n in range(3):
            grad_s[n, cut] = grads[n]
    upward = dot(qw_ref[0], grad_s[0].astype(BF16), ((1,), (0,)))
    upward = upward + dot(qw_ref[1], grad_s[1].astype(BF16), ((1,), (0,)))
    upward = upward + dot(qw_ref[2], grad_s[2].astype(BF16), ((1,), (0,)))
    upward = upward.T
    grad = inverse * (
        upward
        - jnp.mean(upward, axis=1, keepdims=True)
        - low_s[...] * jnp.mean(upward * low_s[...], axis=1, keepdims=True)
    )
    grad = grad.astype(BF16)
    gr_ref[...] = grad.reshape(gr_ref.shape)
    att_s[...] = dot(ow_ref[...], grad, ((1,), (1,)))
    for z in range(count):
        for f, block in enumerate(pack(att_s[z * rows : (z + 1) * rows, :], parts)):
            up_ref[z * parts + f] = block.astype(BF16)


def middle(count, parts, att, res, cot, gains, out_weight, qkv_weight):
    width = out_weight.shape[0]
    vmem = pl.BlockSpec(memory_space=pltpu.VMEM)
    hbm = pl.BlockSpec(memory_space=pl.ANY)
    return pl.pallas_call(
        functools.partial(middle_kernel, count, parts),
        out_shape=[
            jax.ShapeDtypeStruct(res.shape, BF16),
            jax.ShapeDtypeStruct(att.shape, BF16),
        ],
        in_specs=[vmem, vmem, vmem, vmem, hbm, hbm],
        out_specs=[vmem, vmem],
        scratch_shapes=[
            pltpu.VMEM(out_weight.shape, BF16),
            pltpu.VMEM(qkv_weight.shape, BF16),
            pltpu.VMEM((width, LANES), F32),
            pltpu.VMEM((LANES, width), F32),
            pltpu.VMEM((width, LANES), F32),
            pltpu.VMEM((3, width, LANES), F32),
            pltpu.VMEM((3, width, LANES), F32),
            pltpu.SemaphoreType.DMA((4,)),
        ],
        compiler_params=PARAMS,
        name="middle",
    )(att, res, cot, gains, out_weight, qkv_weight)


def swap(array, axis, count, s):
    if s == 0:
        return array
    return lax.ppermute(array, axis, [(n, n ^ s) for n in range(count)])


def local(
    count,
    parts,
    residual,
    spatial_query,
    spatial_key,
    spatial_value,
    out_weight,
    qkv_weight,
    space_gains,
    time_gains,
    cotangent,
):
    tokens, width = residual.shape[1:]
    wide_space = jnp.broadcast_to(space_gains[:, :, None], space_gains.shape + (1,))
    wide_time = jnp.broadcast_to(time_gains[:, :, None], time_gains.shape + (1,))
    own = turn("seq", count, (spatial_query[0], spatial_key[0], spatial_value[0]))
    held = [swap(own[s], "seq", count, s) for s in range(count)]
    frames = (parts, tokens // parts, width)
    res = lax.all_to_all(residual.reshape(frames), "frm", 0, 0, tiled=True)
    cot = lax.all_to_all(cotangent.reshape(frames), "frm", 0, 0, tiled=True)
    sent = space_fwd("seq", parts, wide_space, held)
    att = lax.all_to_all(sent, ("seq", "frm"), 0, 0, tiled=True)
    grad, up = middle(count, parts, att, res, cot, wide_time, out_weight, qkv_weight)
    up = lax.all_to_all(up, ("seq", "frm"), 0, 0, tiled=True)
    grad = lax.all_to_all(grad, "frm", 0, 0, tiled=True)
    grads = space_bwd("seq", parts, wide_space, up, held)
    back = [swap(grads[s], "seq", count, s) for s in range(count)]
    outs = unturn("seq", back)
    return (grad.reshape(residual.shape),) + tuple(out[None] for out in outs)


def solution(mesh):
    tokens = P(("grp", "frm"), "seq", None)
    return jax.shard_map(
        functools.partial(local, mesh.shape["seq"], mesh.shape["frm"]),
        mesh=mesh,
        in_specs=(tokens, tokens, tokens, tokens, P(), P(), P(), P(), tokens),
        out_specs=(tokens, tokens, tokens, tokens),
        check_vma=False,
    )
```

```python
import functools

import jax
import jax.numpy as jnp
from jax import lax
from jax.experimental import pallas as pl
from jax.experimental.pallas import tpu as pltpu
from jax.sharding import PartitionSpec as P

HD = 72
EPS = 1e-06
F32 = jnp.float32
BF16 = jnp.bfloat16
LANES = 128
VMEM_LIMIT = 56 * 1024 * 1024

PARAMS = pltpu.CompilerParams(vmem_limit_bytes=VMEM_LIMIT)


def cost(micros):
    return pl.CostEstimate(flops=int(micros * 1e9), bytes_accessed=0, transcendentals=0)


def dot(left, right, dims):
    return lax.dot_general(left, right, (dims, ((), ())), preferred_element_type=F32)


def rounded(value):
    return value.astype(BF16).astype(F32)


def head_norm(tensor):
    inverse = lax.rsqrt(jnp.mean(tensor * tensor, axis=-2, keepdims=True) + EPS)
    return (tensor * inverse, inverse)


def norm_back(upward, hat, inverse, gain):
    scaled = upward * gain
    return inverse * (scaled - hat * jnp.mean(scaled * hat, axis=-2, keepdims=True))


def exchange_lanes(blocks, width):
    count = len(blocks)
    group = lax.broadcasted_iota(jnp.int32, blocks[0].shape, 1) // width
    results = []
    for a in range(count):
        result = None
        for b in range(count):
            shift = (width * (b - a)) % (width * count)
            moved = blocks[b] if shift == 0 else pltpu.roll(blocks[b], shift, 1)
            result = moved if result is None else jnp.where(group == b, moved, result)
        results.append(result)
    return results


def column(row):
    size = row.shape[1]
    here = lax.broadcasted_iota(jnp.int32, (size, size), 0) == lax.broadcasted_iota(
        jnp.int32, (size, size), 1
    )
    return jnp.sum(jnp.where(here, row, 0.0), axis=1, keepdims=True)


def is_dense(rows, parts):
    return rows % (8 * parts) == 0


def pack(tile, parts):
    rows, width = tile.shape[0], tile.shape[1] // parts
    if is_dense(rows, parts):
        own = rows // parts
        return exchange_lanes([tile[b * own : (b + 1) * own] for b in range(parts)], width)
    return [tile[:, b * width : (b + 1) * width] for b in range(parts)]


def unpack(blocks):
    parts = len(blocks)
    if blocks[0].shape[1] * parts == LANES:
        return jnp.concatenate(blocks, axis=1)
    return jnp.concatenate(exchange_lanes(blocks, blocks[0].shape[1] // parts), axis=0)


def block_shape(rows, parts):
    if is_dense(rows, parts):
        return (rows // parts, LANES)
    return (rows, LANES // parts)


def turn_kernel(axis, q_ref, k_ref, v_ref, res_ref, cot_ref, both_ref, *rest):
    out_refs, held = rest[:-1], rest[-1]
    rows = out_refs[0].shape[1]
    parts, _, own, width = both_ref.shape
    me = lax.axis_index(axis)
    for n, ref in enumerate((res_ref, cot_ref)):
        both_ref[:, n] = ref[...].reshape(parts, own, width)
    for n, ref in enumerate((q_ref, k_ref, v_ref)):
        held[n] = ref[...].T
    for s, ref in enumerate(out_refs):
        start = pl.multiple_of((me ^ s) * rows, rows)
        ref[...] = held[:, pl.ds(start, rows), :]


def turn(axis, count, parts, arrays, frames):
    tokens, width = arrays[0].shape
    outs = pl.pallas_call(
        functools.partial(turn_kernel, axis),
        out_shape=[jax.ShapeDtypeStruct((parts, 2, tokens // parts, width), BF16)]
        + [jax.ShapeDtypeStruct((3, width // count, tokens), BF16)] * count,
        scratch_shapes=[pltpu.VMEM((3, width, tokens), BF16)],
        compiler_params=PARAMS,
        cost_estimate=cost(3),
        name="turn",
    )(*arrays, *frames)
    return outs[0], outs[1:]


def unturn_kernel(axis, grad_ref, *refs):
    in_refs, out_refs, grad_out, held = refs[:-5], refs[-5:-2], refs[-2], refs[-1]
    rows = in_refs[0].shape[1]
    me = lax.axis_index(axis)
    grad_out[...] = grad_ref[...]
    for s, ref in enumerate(in_refs):
        start = pl.multiple_of((me ^ s) * rows, rows)
        held[:, pl.ds(start, rows), :] = ref[...]
    for n, ref in enumerate(out_refs):
        ref[...] = held[n].T


def unturn(axis, grad, blocks):
    count = len(blocks)
    _, rows, tokens = blocks[0].shape
    return pl.pallas_call(
        functools.partial(unturn_kernel, axis),
        out_shape=[jax.ShapeDtypeStruct((tokens, rows * count), BF16)] * 4,
        scratch_shapes=[pltpu.VMEM((3, rows * count, tokens), BF16)],
        compiler_params=PARAMS,
        cost_estimate=cost(3),
        name="unturn",
    )(grad, *blocks)


def gather_part(refs, part):
    return jnp.concatenate([ref[part].astype(F32) for ref in refs], axis=1)


def head_expons(query, key, query_gain, key_gain):
    query_nrm = (head_norm(query)[0] * query_gain).astype(BF16)
    key_nrm = (head_norm(key)[0] * key_gain).astype(BF16)
    expons = jnp.exp(dot(key_nrm, query_nrm, ((0,), (0,))) * (HD ** (-0.5)))
    return expons, 1.0 / jnp.sum(expons, axis=0, keepdims=True)


def space_fwd_kernel(axis, parts, gain_ref, *refs):
    in_refs, out_ref, held = refs[:-2], refs[-2], refs[-1]
    count = len(in_refs)
    rows = in_refs[0].shape[1]
    me = lax.axis_index(axis)
    query, key, value = (gather_part(in_refs, n) for n in range(3))
    query_gain, key_gain = (column(gain_ref[n : n + 1]) for n in range(2))
    for h in range(rows // HD):
        cut = slice(h * HD, (h + 1) * HD)
        expons, scale = head_expons(query[cut], key[cut], query_gain, key_gain)
        attended = dot(value[cut].astype(BF16), expons.astype(BF16), ((1,), (0,)))
        held[cut, :] = attended * scale
    for s in range(count):
        blocks = pack(held[:, s * LANES : (s + 1) * LANES], parts)
        for f, block in enumerate(blocks):
            out_ref[(me ^ s) * parts + f] = block.astype(BF16)


def space_fwd(axis, parts, gains, arrays):
    count = len(arrays)
    _, rows, tokens = arrays[0].shape
    return pl.pallas_call(
        functools.partial(space_fwd_kernel, axis, parts),
        out_shape=jax.ShapeDtypeStruct((count * parts,) + block_shape(rows, parts), BF16),
        scratch_shapes=[pltpu.VMEM((rows, count * tokens), F32)],
        compiler_params=PARAMS,
        cost_estimate=cost(4),
        name="space_fwd",
    )(gains, *arrays)


def space_weights_kernel(gain_ref, *refs):
    in_refs, weight_ref = refs[:-1], refs[-1]
    query, key = (gather_part(in_refs, n) for n in range(2))
    query_gain, key_gain = (column(gain_ref[n : n + 1]) for n in range(2))
    for h in range(weight_ref.shape[0]):
        cut = slice(h * HD, (h + 1) * HD)
        expons, scale = head_expons(query[cut], key[cut], query_gain, key_gain)
        weight_ref[h] = (expons * scale).astype(BF16)


def space_weights(gains, arrays):
    count = len(arrays)
    _, rows, tokens = arrays[0].shape
    return pl.pallas_call(
        space_weights_kernel,
        out_shape=jax.ShapeDtypeStruct((rows // HD, count * tokens, count * tokens), BF16),
        compiler_params=PARAMS,
        cost_estimate=cost(8),
        name="space_weights",
    )(gains, *arrays)


def space_bwd_kernel(axis, parts, gain_ref, weight_ref, up_ref, *refs):
    count = (len(refs) - 1) // 2
    in_refs, out_refs, held = refs[:count], refs[count:-1], refs[-1]
    rows = in_refs[0].shape[1]
    me = lax.axis_index(axis)
    for s in range(count):
        blocks = [up_ref[(me ^ s) * parts + f].astype(F32) for f in range(parts)]
        held[:, s * LANES : (s + 1) * LANES] = unpack(blocks)
    query, key, value = (gather_part(in_refs, n) for n in range(3))
    query_gain, key_gain = (column(gain_ref[n : n + 1]) for n in range(2))
    factor = HD ** (-0.5)
    grads = []
    for h in range(rows // HD):
        cut = slice(h * HD, (h + 1) * HD)
        query_hat, query_inv = head_norm(query[cut])
        key_hat, key_inv = head_norm(key[cut])
        query_nrm = (query_hat * query_gain).astype(BF16)
        key_nrm = (key_hat * key_gain).astype(BF16)
        up = held[cut, :].astype(BF16)
        weights = weight_ref[h]
        shares = weights.astype(F32)
        share_grad = dot(value[cut].astype(BF16), up, ((0,), (0,)))
        centre = jnp.sum(shares * share_grad, axis=0, keepdims=True)
        score_grad = (shares * (share_grad - centre) * factor).astype(BF16)
        query_grad = dot(key_nrm, score_grad, ((1,), (0,)))
        key_grad = dot(query_nrm, score_grad, ((1,), (1,)))
        value_grad = dot(up, weights, ((1,), (1,)))
        grads.append(
            (
                norm_back(query_grad, query_hat, query_inv, query_gain),
                norm_back(key_grad, key_hat, key_inv, key_gain),
                value_grad,
            )
        )
    for n in range(3):
        whole = jnp.concatenate([grad[n] for grad in grads], axis=0).astype(BF16)
        for s in range(count):
            out_refs[s][n] = whole[:, s * LANES : (s + 1) * LANES]


def space_bwd(axis, parts, gains, weights, up, arrays):
    count = len(arrays)
    _, rows, tokens = arrays[0].shape
    return pl.pallas_call(
        functools.partial(space_bwd_kernel, axis, parts),
        out_shape=[jax.ShapeDtypeStruct((3, rows, tokens), BF16)] * count,
        scratch_shapes=[pltpu.VMEM((rows, count * tokens), F32)],
        compiler_params=PARAMS,
        cost_estimate=cost(6),
        name="space_bwd",
    )(gains, weights, up, *arrays)


def time_head(query_in, key_in, value, upward, query_gain, key_gain, parts):
    width = LANES // parts
    factor = HD ** (-0.5)
    query_hat, query_inv = head_norm(query_in)
    key_hat, key_inv = head_norm(key_in)
    query_nrm = rounded(query_hat * query_gain)
    key_nrm = rounded(key_hat * key_gain)

    def turned(tensor, r):
        shift = (r * width) % LANES
        return tensor if shift == 0 else pltpu.roll(tensor, shift, 1)

    keys = [turned(key_nrm, r) for r in range(parts)]
    expons = [jnp.exp(jnp.sum(query_nrm * keys[r], axis=0, keepdims=True) * factor) for r in range(parts)]
    scale = 1.0 / functools.reduce(jnp.add, expons)
    shares = [expon * scale for expon in expons]
    share_grads = [jnp.sum(upward * turned(value, r), axis=0, keepdims=True) for r in range(parts)]
    centre = functools.reduce(jnp.add, [a * b for a, b in zip(shares, share_grads)])
    score_grads = [rounded(shares[r] * (share_grads[r] - centre) * factor) for r in range(parts)]
    query_grad = functools.reduce(jnp.add, [score_grads[r] * keys[r] for r in range(parts)])
    key_grad = functools.reduce(jnp.add, [turned(score_grads[r] * query_nrm, -r) for r in range(parts)])
    value_grad = functools.reduce(jnp.add, [turned(rounded(shares[r]) * upward, -r) for r in range(parts)])
    return (
        norm_back(query_grad, query_hat, query_inv, query_gain),
        norm_back(key_grad, key_hat, key_inv, key_gain),
        value_grad,
    )


def middle_kernel(
    count,
    parts,
    att_ref,
    pair_ref,
    gain_ref,
    ow_hbm,
    qw_hbm,
    gr_ref,
    up_ref,
    ow_ref,
    qw_ref,
    att_s,
    low_s,
    cot_s,
    qkv_s,
    grad_s,
    sems,
):
    width = ow_ref.shape[0]
    rows = width // count
    copies = [pltpu.make_async_copy(ow_hbm, ow_ref, sems.at[0])]
    copies += [pltpu.make_async_copy(qw_hbm.at[n], qw_ref.at[n], sems.at[1 + n]) for n in range(3)]
    for copy in copies:
        copy.start()
    for z in range(count):
        att_s[z * rows : (z + 1) * rows, :] = unpack(
            [att_ref[z * parts + f].astype(F32) for f in range(parts)]
        )
    attended = att_s[...].T.astype(BF16)
    cot_s[...] = pair_ref[:, 1].reshape(LANES, width).astype(F32).T
    copies[0].wait()
    mixed = rounded(
        pair_ref[:, 0].reshape(LANES, width).astype(F32) + dot(attended, ow_ref[...], ((1,), (0,)))
    )
    centred = mixed - jnp.mean(mixed, axis=1, keepdims=True)
    inverse = lax.rsqrt(jnp.mean(centred * centred, axis=1, keepdims=True) + EPS)
    normed = centred * inverse
    low_s[...] = normed
    lowered = normed.astype(BF16)
    for n in range(3):
        copies[1 + n].wait()
        product = rounded(dot(lowered, qw_ref[n], ((1,), (0,))))
        qkv_s[n] = product.T
    query_gain, key_gain = (column(gain_ref[n : n + 1]) for n in range(2))
    for h in range(width // HD):
        cut = slice(h * HD, (h + 1) * HD)
        grads = time_head(
            qkv_s[0, cut], qkv_s[1, cut], qkv_s[2, cut], cot_s[cut], query_gain, key_gain, parts
        )
        for n in range(3):
            grad_s[n, cut] = grads[n]
    upward = dot(qw_ref[0], grad_s[0].astype(BF16), ((1,), (0,)))
    upward = upward + dot(qw_ref[1], grad_s[1].astype(BF16), ((1,), (0,)))
    upward = upward + dot(qw_ref[2], grad_s[2].astype(BF16), ((1,), (0,)))
    upward = upward.T
    grad = inverse * (
        upward
        - jnp.mean(upward, axis=1, keepdims=True)
        - low_s[...] * jnp.mean(upward * low_s[...], axis=1, keepdims=True)
    )
    grad = grad.astype(BF16)
    gr_ref[...] = grad.reshape(gr_ref.shape)
    att_s[...] = dot(ow_ref[...], grad, ((1,), (1,)))
    for z in range(count):
        for f, block in enumerate(pack(att_s[z * rows : (z + 1) * rows, :], parts)):
            up_ref[z * parts + f] = block.astype(BF16)


def middle(count, parts, att, pair, gains, out_weight, qkv_weight):
    width = out_weight.shape[0]
    vmem = pl.BlockSpec(memory_space=pltpu.VMEM)
    hbm = pl.BlockSpec(memory_space=pl.ANY)
    return pl.pallas_call(
        functools.partial(middle_kernel, count, parts),
        out_shape=[
            jax.ShapeDtypeStruct((pair.shape[0],) + pair.shape[2:], BF16),
            jax.ShapeDtypeStruct(att.shape, BF16),
        ],
        in_specs=[vmem, vmem, vmem, hbm, hbm],
        out_specs=[vmem, vmem],
        scratch_shapes=[
            pltpu.VMEM(out_weight.shape, BF16),
            pltpu.VMEM(qkv_weight.shape, BF16),
            pltpu.VMEM((width, LANES), F32),
            pltpu.VMEM((LANES, width), F32),
            pltpu.VMEM((width, LANES), F32),
            pltpu.VMEM((3, width, LANES), F32),
            pltpu.VMEM((3, width, LANES), F32),
            pltpu.SemaphoreType.DMA((4,)),
        ],
        compiler_params=PARAMS,
        cost_estimate=cost(10),
        name="middle",
    )(att, pair, gains, out_weight, qkv_weight)


def swap(array, axis, count, s):
    if s == 0:
        return array
    return lax.ppermute(array, axis, [(n, n ^ s) for n in range(count)])


def local(
    count,
    parts,
    residual,
    spatial_query,
    spatial_key,
    spatial_value,
    out_weight,
    qkv_weight,
    space_gains,
    time_gains,
    cotangent,
):
    tokens, width = residual.shape[1:]
    both, own = turn(
        "seq",
        count,
        parts,
        (spatial_query[0], spatial_key[0], spatial_value[0]),
        (residual[0], cotangent[0]),
    )
    held = [swap(own[s], "seq", count, s) for s in range(count)]
    both = lax.all_to_all(both, "frm", 0, 0, tiled=True)
    sent = space_fwd("seq", parts, space_gains, held)
    att = lax.all_to_all(sent, ("seq", "frm"), 0, 0, tiled=True)
    late = lax.optimization_barrier((sent, *held))[1:]
    weights = space_weights(space_gains, late)
    att, both, weights = lax.optimization_barrier((att, both, weights))
    grad, up = middle(count, parts, att, both, time_gains, out_weight, qkv_weight)
    up = lax.all_to_all(up, ("seq", "frm"), 0, 0, tiled=True)
    grads = space_bwd("seq", parts, space_gains, weights, up, held)
    back = [swap(grads[s], "seq", count, s) for s in range(count)]
    grad, _ = lax.optimization_barrier((grad, back[1]))
    grad = lax.all_to_all(grad, "frm", 0, 0, tiled=True)
    grad_query, grad_key, grad_value, grad = unturn(
        "seq", grad.reshape((tokens, width)), back
    )
    return (grad[None], grad_query[None], grad_key[None], grad_value[None])


def solution(mesh):
    tokens = P(("grp", "frm"), "seq", None)
    return jax.shard_map(
        functools.partial(local, mesh.shape["seq"], mesh.shape["frm"]),
        mesh=mesh,
        in_specs=(tokens, tokens, tokens, tokens, P(), P(), P(), P(), tokens),
        out_specs=(tokens, tokens, tokens, tokens),
        check_vma=False,
    )
```

```python
import functools

import jax
import jax.numpy as jnp
from jax import lax
from jax.experimental import pallas as pl
from jax.experimental.pallas import tpu as pltpu
from jax.sharding import PartitionSpec as P

HD = 72
EPS = 1e-06
F32 = jnp.float32
BF16 = jnp.bfloat16
LANES = 128
VMEM_LIMIT = 40 * 1024 * 1024

PARAMS = pltpu.CompilerParams(vmem_limit_bytes=VMEM_LIMIT)


def in_hbm(array):
    return pltpu.with_memory_space_constraint(array, pltpu.HBM)


def cost(micros):
    return pl.CostEstimate(flops=int(micros * 1e9), bytes_accessed=0, transcendentals=0)


def dot(left, right, dims):
    return lax.dot_general(left, right, (dims, ((), ())), preferred_element_type=F32)


def rounded(value):
    return value.astype(BF16).astype(F32)


def head_norm(tensor):
    inverse = lax.rsqrt(jnp.mean(tensor * tensor, axis=-2, keepdims=True) + EPS)
    return (tensor * inverse, inverse)


def norm_back(upward, hat, inverse, gain):
    scaled = upward * gain
    return inverse * (scaled - hat * jnp.mean(scaled * hat, axis=-2, keepdims=True))


def exchange_lanes(blocks, width):
    count = len(blocks)
    group = lax.broadcasted_iota(jnp.int32, blocks[0].shape, 1) // width
    results = []
    for a in range(count):
        result = None
        for b in range(count):
            shift = (width * (b - a)) % (width * count)
            moved = blocks[b] if shift == 0 else pltpu.roll(blocks[b], shift, 1)
            result = moved if result is None else jnp.where(group == b, moved, result)
        results.append(result)
    return results


def column(row):
    size = row.shape[1]
    here = lax.broadcasted_iota(jnp.int32, (size, size), 0) == lax.broadcasted_iota(
        jnp.int32, (size, size), 1
    )
    return jnp.sum(jnp.where(here, row, 0.0), axis=1, keepdims=True)


def is_dense(rows, parts):
    return rows % (8 * parts) == 0


def pack(tile, parts):
    rows, width = tile.shape[0], tile.shape[1] // parts
    if is_dense(rows, parts):
        own = rows // parts
        return exchange_lanes([tile[b * own : (b + 1) * own] for b in range(parts)], width)
    return [tile[:, b * width : (b + 1) * width] for b in range(parts)]


def unpack(blocks):
    parts = len(blocks)
    if blocks[0].shape[1] * parts == LANES:
        return jnp.concatenate(blocks, axis=1)
    return jnp.concatenate(exchange_lanes(blocks, blocks[0].shape[1] // parts), axis=0)


def block_shape(rows, parts):
    if is_dense(rows, parts):
        return (rows // parts, LANES)
    return (rows, LANES // parts)


def turn_kernel(axis, *refs):
    in_refs, both_ref, out_refs = refs[:5], refs[5], refs[6:-3]
    landed, held, sems = refs[-3:]
    rows = out_refs[0].shape[1]
    parts, _, own, width = both_ref.shape
    me = lax.axis_index(axis)
    copies = [pltpu.make_async_copy(ref, landed.at[n], sems.at[n]) for n, ref in enumerate(in_refs)]
    for copy in copies:
        copy.start()
    for n in range(3):
        copies[n].wait()
        held[n] = landed[n].T
    for n in range(2):
        copies[3 + n].wait()
        both_ref[:, n] = landed[3 + n].reshape(parts, own, width)
    for s, ref in enumerate(out_refs):
        start = pl.multiple_of((me ^ s) * rows, rows)
        ref[...] = held[:, pl.ds(start, rows), :]


def turn(axis, count, parts, arrays, frames):
    tokens, width = arrays[0].shape
    outs = pl.pallas_call(
        functools.partial(turn_kernel, axis),
        out_shape=[jax.ShapeDtypeStruct((parts, 2, tokens // parts, width), BF16)]
        + [jax.ShapeDtypeStruct((3, width // count, tokens), BF16)] * count,
        in_specs=[pl.BlockSpec(memory_space=pltpu.HBM)] * 5,
        scratch_shapes=[
            pltpu.VMEM((5, tokens, width), BF16),
            pltpu.VMEM((3, width, tokens), BF16),
            pltpu.SemaphoreType.DMA((5,)),
        ],
        compiler_params=PARAMS,
        cost_estimate=cost(3),
        name="turn",
    )(*(in_hbm(array) for array in (*arrays, *frames)))
    return outs[0], outs[1:]


def unturn_kernel(axis, grad_ref, *refs):
    in_refs, out_refs, grad_out, held = refs[:-5], refs[-5:-2], refs[-2], refs[-1]
    rows = in_refs[0].shape[1]
    me = lax.axis_index(axis)
    grad_out[...] = grad_ref[...]
    for s, ref in enumerate(in_refs):
        start = pl.multiple_of((me ^ s) * rows, rows)
        held[:, pl.ds(start, rows), :] = ref[...]
    for n, ref in enumerate(out_refs):
        ref[...] = held[n].T


def unturn(axis, grad, blocks):
    count = len(blocks)
    _, rows, tokens = blocks[0].shape
    return pl.pallas_call(
        functools.partial(unturn_kernel, axis),
        out_shape=[jax.ShapeDtypeStruct((tokens, rows * count), BF16)] * 4,
        scratch_shapes=[pltpu.VMEM((3, rows * count, tokens), BF16)],
        compiler_params=PARAMS,
        cost_estimate=cost(3),
        name="unturn",
    )(grad, *blocks)


def gather_part(refs, part):
    return jnp.concatenate([ref[part].astype(F32) for ref in refs], axis=1)


def head_expons(query, key, query_gain, key_gain):
    query_nrm = (head_norm(query)[0] * query_gain).astype(BF16)
    key_nrm = (head_norm(key)[0] * key_gain).astype(BF16)
    expons = jnp.exp(dot(key_nrm, query_nrm, ((0,), (0,))) * (HD ** (-0.5)))
    return expons, 1.0 / jnp.sum(expons, axis=0, keepdims=True)


def space_fwd_kernel(axis, parts, gain_ref, *refs):
    in_refs, out_ref, held = refs[:-2], refs[-2], refs[-1]
    count = len(in_refs)
    rows = in_refs[0].shape[1]
    me = lax.axis_index(axis)
    query, key, value = (gather_part(in_refs, n) for n in range(3))
    query_gain, key_gain = (column(gain_ref[n : n + 1]) for n in range(2))
    for h in range(rows // HD):
        cut = slice(h * HD, (h + 1) * HD)
        expons, scale = head_expons(query[cut], key[cut], query_gain, key_gain)
        attended = dot(value[cut].astype(BF16), expons.astype(BF16), ((1,), (0,)))
        held[cut, :] = attended * scale
    for s in range(count):
        blocks = pack(held[:, s * LANES : (s + 1) * LANES], parts)
        for f, block in enumerate(blocks):
            out_ref[(me ^ s) * parts + f] = block.astype(BF16)


def space_fwd(axis, parts, gains, arrays):
    count = len(arrays)
    _, rows, tokens = arrays[0].shape
    return pl.pallas_call(
        functools.partial(space_fwd_kernel, axis, parts),
        out_shape=jax.ShapeDtypeStruct((count * parts,) + block_shape(rows, parts), BF16),
        scratch_shapes=[pltpu.VMEM((rows, count * tokens), F32)],
        compiler_params=PARAMS,
        cost_estimate=cost(4),
        name="space_fwd",
    )(gains, *arrays)


def space_weights_kernel(gain_ref, *refs):
    in_refs, weight_ref = refs[:-1], refs[-1]
    query, key = (gather_part(in_refs, n) for n in range(2))
    query_gain, key_gain = (column(gain_ref[n : n + 1]) for n in range(2))
    for h in range(weight_ref.shape[0]):
        cut = slice(h * HD, (h + 1) * HD)
        expons, scale = head_expons(query[cut], key[cut], query_gain, key_gain)
        weight_ref[h] = (expons * scale).astype(BF16)


def space_weights(gains, arrays):
    count = len(arrays)
    _, rows, tokens = arrays[0].shape
    return pl.pallas_call(
        space_weights_kernel,
        out_shape=jax.ShapeDtypeStruct((rows // HD, count * tokens, count * tokens), BF16),
        compiler_params=PARAMS,
        cost_estimate=cost(8),
        name="space_weights",
    )(gains, *arrays)


def space_bwd_kernel(axis, parts, gain_ref, weight_ref, up_ref, *refs):
    count = (len(refs) - 1) // 2
    in_refs, out_refs, held = refs[:count], refs[count:-1], refs[-1]
    rows = in_refs[0].shape[1]
    me = lax.axis_index(axis)
    for s in range(count):
        blocks = [up_ref[(me ^ s) * parts + f].astype(F32) for f in range(parts)]
        held[:, s * LANES : (s + 1) * LANES] = unpack(blocks)
    query, key, value = (gather_part(in_refs, n) for n in range(3))
    query_gain, key_gain = (column(gain_ref[n : n + 1]) for n in range(2))
    factor = HD ** (-0.5)
    grads = []
    for h in range(rows // HD):
        cut = slice(h * HD, (h + 1) * HD)
        query_hat, query_inv = head_norm(query[cut])
        key_hat, key_inv = head_norm(key[cut])
        query_nrm = (query_hat * query_gain).astype(BF16)
        key_nrm = (key_hat * key_gain).astype(BF16)
        up = held[cut, :].astype(BF16)
        weights = weight_ref[h]
        shares = weights.astype(F32)
        share_grad = dot(value[cut].astype(BF16), up, ((0,), (0,)))
        centre = jnp.sum(shares * share_grad, axis=0, keepdims=True)
        score_grad = (shares * (share_grad - centre) * factor).astype(BF16)
        query_grad = dot(key_nrm, score_grad, ((1,), (0,)))
        key_grad = dot(query_nrm, score_grad, ((1,), (1,)))
        value_grad = dot(up, weights, ((1,), (1,)))
        grads.append(
            (
                norm_back(query_grad, query_hat, query_inv, query_gain),
                norm_back(key_grad, key_hat, key_inv, key_gain),
                value_grad,
            )
        )
    for n in range(3):
        whole = jnp.concatenate([grad[n] for grad in grads], axis=0).astype(BF16)
        for s in range(count):
            out_refs[s][n] = whole[:, s * LANES : (s + 1) * LANES]


def space_bwd(axis, parts, gains, weights, up, arrays):
    count = len(arrays)
    _, rows, tokens = arrays[0].shape
    return pl.pallas_call(
        functools.partial(space_bwd_kernel, axis, parts),
        out_shape=[jax.ShapeDtypeStruct((3, rows, tokens), BF16)] * count,
        scratch_shapes=[pltpu.VMEM((rows, count * tokens), F32)],
        compiler_params=PARAMS,
        cost_estimate=cost(6),
        name="space_bwd",
    )(gains, weights, up, *arrays)


def time_head(query_in, key_in, value, upward, query_gain, key_gain, parts):
    width = LANES // parts
    factor = HD ** (-0.5)
    query_hat, query_inv = head_norm(query_in)
    key_hat, key_inv = head_norm(key_in)
    query_nrm = rounded(query_hat * query_gain)
    key_nrm = rounded(key_hat * key_gain)

    def turned(tensor, r):
        shift = (r * width) % LANES
        return tensor if shift == 0 else pltpu.roll(tensor, shift, 1)

    keys = [turned(key_nrm, r) for r in range(parts)]
    expons = [jnp.exp(jnp.sum(query_nrm * keys[r], axis=0, keepdims=True) * factor) for r in range(parts)]
    scale = 1.0 / functools.reduce(jnp.add, expons)
    shares = [expon * scale for expon in expons]
    share_grads = [jnp.sum(upward * turned(value, r), axis=0, keepdims=True) for r in range(parts)]
    centre = functools.reduce(jnp.add, [a * b for a, b in zip(shares, share_grads)])
    score_grads = [rounded(shares[r] * (share_grads[r] - centre) * factor) for r in range(parts)]
    query_grad = functools.reduce(jnp.add, [score_grads[r] * keys[r] for r in range(parts)])
    key_grad = functools.reduce(jnp.add, [turned(score_grads[r] * query_nrm, -r) for r in range(parts)])
    value_grad = functools.reduce(jnp.add, [turned(rounded(shares[r]) * upward, -r) for r in range(parts)])
    return (
        norm_back(query_grad, query_hat, query_inv, query_gain),
        norm_back(key_grad, key_hat, key_inv, key_gain),
        value_grad,
    )


def middle_kernel(
    count,
    parts,
    att_ref,
    pair_ref,
    gain_ref,
    ow_hbm,
    qw_hbm,
    gr_ref,
    up_ref,
    ow_ref,
    qw_ref,
    att_s,
    low_s,
    cot_s,
    qkv_s,
    grad_s,
    sems,
):
    width = ow_ref.shape[0]
    rows = width // count
    copies = [pltpu.make_async_copy(ow_hbm, ow_ref, sems.at[0])]
    copies += [pltpu.make_async_copy(qw_hbm.at[n], qw_ref.at[n], sems.at[1 + n]) for n in range(3)]
    for copy in copies:
        copy.start()
    for z in range(count):
        att_s[z * rows : (z + 1) * rows, :] = unpack(
            [att_ref[z * parts + f].astype(F32) for f in range(parts)]
        )
    attended = att_s[...].T.astype(BF16)
    cot_s[...] = pair_ref[:, 1].reshape(LANES, width).astype(F32).T
    copies[0].wait()
    mixed = rounded(
        pair_ref[:, 0].reshape(LANES, width).astype(F32) + dot(attended, ow_ref[...], ((1,), (0,)))
    )
    centred = mixed - jnp.mean(mixed, axis=1, keepdims=True)
    inverse = lax.rsqrt(jnp.mean(centred * centred, axis=1, keepdims=True) + EPS)
    normed = centred * inverse
    low_s[...] = normed
    lowered = normed.astype(BF16)
    for n in range(3):
        copies[1 + n].wait()
        product = rounded(dot(lowered, qw_ref[n], ((1,), (0,))))
        qkv_s[n] = product.T
    query_gain, key_gain = (column(gain_ref[n : n + 1]) for n in range(2))
    for h in range(width // HD):
        cut = slice(h * HD, (h + 1) * HD)
        grads = time_head(
            qkv_s[0, cut], qkv_s[1, cut], qkv_s[2, cut], cot_s[cut], query_gain, key_gain, parts
        )
        for n in range(3):
            grad_s[n, cut] = grads[n]
    upward = dot(qw_ref[0], grad_s[0].astype(BF16), ((1,), (0,)))
    upward = upward + dot(qw_ref[1], grad_s[1].astype(BF16), ((1,), (0,)))
    upward = upward + dot(qw_ref[2], grad_s[2].astype(BF16), ((1,), (0,)))
    upward = upward.T
    grad = inverse * (
        upward
        - jnp.mean(upward, axis=1, keepdims=True)
        - low_s[...] * jnp.mean(upward * low_s[...], axis=1, keepdims=True)
    )
    grad = grad.astype(BF16)
    gr_ref[...] = grad.reshape(gr_ref.shape)
    att_s[...] = dot(ow_ref[...], grad, ((1,), (1,)))
    for z in range(count):
        for f, block in enumerate(pack(att_s[z * rows : (z + 1) * rows, :], parts)):
            up_ref[z * parts + f] = block.astype(BF16)


def middle(count, parts, att, pair, gains, out_weight, qkv_weight):
    width = out_weight.shape[0]
    vmem = pl.BlockSpec(memory_space=pltpu.VMEM)
    return pl.pallas_call(
        functools.partial(middle_kernel, count, parts),
        out_shape=[
            jax.ShapeDtypeStruct((pair.shape[0],) + pair.shape[2:], BF16),
            jax.ShapeDtypeStruct(att.shape, BF16),
        ],
        in_specs=[vmem] * 3 + [pl.BlockSpec(memory_space=pltpu.HBM)] * 2,
        out_specs=[vmem, vmem],
        scratch_shapes=[
            pltpu.VMEM(out_weight.shape, BF16),
            pltpu.VMEM(qkv_weight.shape, BF16),
            pltpu.VMEM((width, LANES), F32),
            pltpu.VMEM((LANES, width), F32),
            pltpu.VMEM((width, LANES), F32),
            pltpu.VMEM((3, width, LANES), F32),
            pltpu.VMEM((3, width, LANES), F32),
            pltpu.SemaphoreType.DMA((4,)),
        ],
        compiler_params=PARAMS,
        cost_estimate=cost(10),
        name="middle",
    )(att, pair, gains, in_hbm(out_weight), in_hbm(qkv_weight))


def swap(array, axis, count, s):
    if s == 0:
        return array
    return lax.ppermute(array, axis, [(n, n ^ s) for n in range(count)])


def local(
    count,
    parts,
    residual,
    spatial_query,
    spatial_key,
    spatial_value,
    out_weight,
    qkv_weight,
    space_gains,
    time_gains,
    cotangent,
):
    tokens, width = residual.shape[1:]
    both, own = turn(
        "seq",
        count,
        parts,
        (spatial_query[0], spatial_key[0], spatial_value[0]),
        (residual[0], cotangent[0]),
    )
    held = [swap(own[s], "seq", count, s) for s in range(count)]
    both = lax.all_to_all(both, "frm", 0, 0, tiled=True)
    sent = space_fwd("seq", parts, space_gains, held)
    att = lax.all_to_all(sent, ("seq", "frm"), 0, 0, tiled=True)
    late = lax.optimization_barrier((sent, *held))[1:]
    weights = space_weights(space_gains, late)
    att, both, weights = lax.optimization_barrier((att, both, weights))
    grad, up = middle(count, parts, att, both, time_gains, out_weight, qkv_weight)
    up = lax.all_to_all(up, ("seq", "frm"), 0, 0, tiled=True)
    grads = space_bwd("seq", parts, space_gains, weights, up, held)
    back = [swap(grads[s], "seq", count, s) for s in range(count)]
    grad, _ = lax.optimization_barrier((grad, back[1]))
    grad = lax.all_to_all(grad, "frm", 0, 0, tiled=True)
    grad_query, grad_key, grad_value, grad = unturn(
        "seq", grad.reshape((tokens, width)), back
    )
    return (grad[None], grad_query[None], grad_key[None], grad_value[None])


def solution(mesh):
    tokens = P(("grp", "frm"), "seq", None)
    return jax.shard_map(
        functools.partial(local, mesh.shape["seq"], mesh.shape["frm"]),
        mesh=mesh,
        in_specs=(tokens, tokens, tokens, tokens, P(), P(), P(), P(), tokens),
        out_specs=(tokens, tokens, tokens, tokens),
        check_vma=False,
    )
```

```python
import functools

import jax
import jax.numpy as jnp
from jax import lax
from jax.experimental import pallas as pl
from jax.experimental.pallas import tpu as pltpu
from jax.sharding import PartitionSpec as P

HD = 72
EPS = 1e-06
F32 = jnp.float32
BF16 = jnp.bfloat16
LANES = 128
VMEM_LIMIT = 40 * 1024 * 1024

PARAMS = pltpu.CompilerParams(vmem_limit_bytes=VMEM_LIMIT)


def in_hbm(array):
    return pltpu.with_memory_space_constraint(array, pltpu.HBM)


def cost(micros):
    return pl.CostEstimate(flops=int(micros * 1e9), bytes_accessed=0, transcendentals=0)


def dot(left, right, dims):
    return lax.dot_general(left, right, (dims, ((), ())), preferred_element_type=F32)


def rounded(value):
    return value.astype(BF16).astype(F32)


def head_norm(tensor):
    inverse = lax.rsqrt(jnp.mean(tensor * tensor, axis=-2, keepdims=True) + EPS)
    return (tensor * inverse, inverse)


def norm_back(upward, hat, inverse, gain):
    scaled = upward * gain
    return inverse * (scaled - hat * jnp.mean(scaled * hat, axis=-2, keepdims=True))


def exchange_lanes(blocks, width):
    count = len(blocks)
    group = lax.broadcasted_iota(jnp.int32, blocks[0].shape, 1) // width
    results = []
    for a in range(count):
        result = None
        for b in range(count):
            shift = (width * (b - a)) % (width * count)
            moved = blocks[b] if shift == 0 else pltpu.roll(blocks[b], shift, 1)
            result = moved if result is None else jnp.where(group == b, moved, result)
        results.append(result)
    return results


def column(row):
    size = row.shape[1]
    here = lax.broadcasted_iota(jnp.int32, (size, size), 0) == lax.broadcasted_iota(
        jnp.int32, (size, size), 1
    )
    return jnp.sum(jnp.where(here, row, 0.0), axis=1, keepdims=True)


def is_dense(rows, parts):
    return rows % (8 * parts) == 0


def pack(tile, parts):
    rows, width = tile.shape[0], tile.shape[1] // parts
    if is_dense(rows, parts):
        own = rows // parts
        return exchange_lanes([tile[b * own : (b + 1) * own] for b in range(parts)], width)
    return [tile[:, b * width : (b + 1) * width] for b in range(parts)]


def unpack(blocks):
    parts = len(blocks)
    if blocks[0].shape[1] * parts == LANES:
        return jnp.concatenate(blocks, axis=1)
    return jnp.concatenate(exchange_lanes(blocks, blocks[0].shape[1] // parts), axis=0)


def block_shape(rows, parts):
    if is_dense(rows, parts):
        return (rows // parts, LANES)
    return (rows, LANES // parts)


def turn_kernel(axis, *refs):
    in_refs, both_ref, out_refs = refs[:5], refs[5], refs[6:-3]
    landed, held, sems = refs[-3:]
    rows = out_refs[0].shape[1]
    parts, _, own, width = both_ref.shape
    me = lax.axis_index(axis)
    copies = [pltpu.make_async_copy(ref, landed.at[n], sems.at[n]) for n, ref in enumerate(in_refs)]
    for copy in copies:
        copy.start()
    for n in range(3):
        copies[n].wait()
        held[n] = landed[n].T
    for n in range(2):
        copies[3 + n].wait()
        both_ref[:, n] = landed[3 + n].reshape(parts, own, width)
    for s, ref in enumerate(out_refs):
        start = pl.multiple_of((me ^ s) * rows, rows)
        ref[...] = held[:, pl.ds(start, rows), :]


def turn(axis, count, parts, arrays, frames):
    tokens, width = arrays[0].shape
    outs = pl.pallas_call(
        functools.partial(turn_kernel, axis),
        out_shape=[jax.ShapeDtypeStruct((parts, 2, tokens // parts, width), BF16)]
        + [jax.ShapeDtypeStruct((3, width // count, tokens), BF16)] * count,
        in_specs=[pl.BlockSpec(memory_space=pltpu.HBM)] * 5,
        scratch_shapes=[
            pltpu.VMEM((5, tokens, width), BF16),
            pltpu.VMEM((3, width, tokens), BF16),
            pltpu.SemaphoreType.DMA((5,)),
        ],
        compiler_params=PARAMS,
        cost_estimate=cost(3),
        name="turn",
    )(*(in_hbm(array) for array in (*arrays, *frames)))
    return outs[0], outs[1:]


def unturn_kernel(axis, frame_axis, count, *refs):
    in_refs, frame_refs = refs[:count], refs[count:-5]
    out_refs, grad_out, held = refs[-5:-2], refs[-2], refs[-1]
    rows = in_refs[0].shape[1]
    me, mine = lax.axis_index(axis), lax.axis_index(frame_axis)
    for s, ref in enumerate(frame_refs):
        grad_out[mine ^ s] = ref[...]
    for s, ref in enumerate(in_refs):
        start = pl.multiple_of((me ^ s) * rows, rows)
        held[:, pl.ds(start, rows), :] = ref[...]
    for n, ref in enumerate(out_refs):
        ref[...] = held[n].T


def unturn(axis, frame_axis, blocks, frame_blocks):
    count = len(blocks)
    _, rows, tokens = blocks[0].shape
    return pl.pallas_call(
        functools.partial(unturn_kernel, axis, frame_axis, count),
        out_shape=[jax.ShapeDtypeStruct((tokens, rows * count), BF16)] * 3
        + [jax.ShapeDtypeStruct((len(frame_blocks),) + frame_blocks[0].shape, BF16)],
        scratch_shapes=[pltpu.VMEM((3, rows * count, tokens), BF16)],
        compiler_params=PARAMS,
        cost_estimate=cost(3),
        name="unturn",
    )(*blocks, *frame_blocks)


def gather_part(refs, part):
    return jnp.concatenate([ref[part].astype(F32) for ref in refs], axis=1)


def head_expons(query, key, query_gain, key_gain):
    query_nrm = (head_norm(query)[0] * query_gain).astype(BF16)
    key_nrm = (head_norm(key)[0] * key_gain).astype(BF16)
    expons = jnp.exp(dot(key_nrm, query_nrm, ((0,), (0,))) * (HD ** (-0.5)))
    return expons, 1.0 / jnp.sum(expons, axis=0, keepdims=True)


def space_fwd_kernel(axis, parts, gain_ref, *refs):
    in_refs, out_ref, held = refs[:-2], refs[-2], refs[-1]
    count = len(in_refs)
    rows = in_refs[0].shape[1]
    me = lax.axis_index(axis)
    query, key, value = (gather_part(in_refs, n) for n in range(3))
    query_gain, key_gain = (column(gain_ref[n : n + 1]) for n in range(2))
    for h in range(rows // HD):
        cut = slice(h * HD, (h + 1) * HD)
        expons, scale = head_expons(query[cut], key[cut], query_gain, key_gain)
        attended = dot(value[cut].astype(BF16), expons.astype(BF16), ((1,), (0,)))
        held[cut, :] = attended * scale
    for s in range(count):
        blocks = pack(held[:, s * LANES : (s + 1) * LANES], parts)
        for f, block in enumerate(blocks):
            out_ref[(me ^ s) * parts + f] = block.astype(BF16)


def space_fwd(axis, parts, gains, arrays):
    count = len(arrays)
    _, rows, tokens = arrays[0].shape
    return pl.pallas_call(
        functools.partial(space_fwd_kernel, axis, parts),
        out_shape=jax.ShapeDtypeStruct((count * parts,) + block_shape(rows, parts), BF16),
        scratch_shapes=[pltpu.VMEM((rows, count * tokens), F32)],
        compiler_params=PARAMS,
        cost_estimate=cost(4),
        name="space_fwd",
    )(gains, *arrays)


def space_weights_kernel(gain_ref, *refs):
    in_refs, weight_ref, att_ref = refs[:-2], refs[-2], refs[-1]
    query, key, value = (gather_part(in_refs, n) for n in range(3))
    query_gain, key_gain = (column(gain_ref[n : n + 1]) for n in range(2))
    for h in range(weight_ref.shape[0]):
        cut = slice(h * HD, (h + 1) * HD)
        expons, scale = head_expons(query[cut], key[cut], query_gain, key_gain)
        weights = (expons * scale).astype(BF16)
        weight_ref[h] = weights
        att_ref[cut, :] = dot(value[cut].astype(BF16), weights, ((1,), (0,)))


def space_weights(gains, arrays):
    count = len(arrays)
    _, rows, tokens = arrays[0].shape
    return pl.pallas_call(
        space_weights_kernel,
        out_shape=[
            jax.ShapeDtypeStruct((rows // HD, count * tokens, count * tokens), BF16),
            jax.ShapeDtypeStruct((rows, count * tokens), F32),
        ],
        compiler_params=PARAMS,
        cost_estimate=cost(8),
        name="space_weights",
    )(gains, *arrays)


def space_bwd_kernel(axis, parts, gain_ref, weight_ref, att_ref, up_ref, *refs):
    count = (len(refs) - 1) // 2
    in_refs, out_refs, held = refs[:count], refs[count:-1], refs[-1]
    rows = in_refs[0].shape[1]
    me = lax.axis_index(axis)
    for s in range(count):
        blocks = [up_ref[(me ^ s) * parts + f].astype(F32) for f in range(parts)]
        held[:, s * LANES : (s + 1) * LANES] = unpack(blocks)
    query, key, value = (gather_part(in_refs, n) for n in range(3))
    query_gain, key_gain = (column(gain_ref[n : n + 1]) for n in range(2))
    factor = HD ** (-0.5)
    extra = lax.broadcasted_iota(jnp.int32, (8, query.shape[1]), 0)
    ones = jnp.where(extra < 2, 1.0, 0.0)
    grads = []
    for h in range(rows // HD):
        cut = slice(h * HD, (h + 1) * HD)
        query_hat, query_inv = head_norm(query[cut])
        key_hat, key_inv = head_norm(key[cut])
        query_nrm = (query_hat * query_gain).astype(BF16)
        key_nrm = (key_hat * key_gain).astype(BF16)
        up_wide = held[cut, :]
        up = up_wide.astype(BF16)
        weights = weight_ref[h]
        centre = jnp.sum(up_wide * att_ref[cut, :], axis=0, keepdims=True)
        high = rounded(centre)
        rows_in = jnp.where(extra == 0, -high, jnp.where(extra == 1, high - centre, 0.0))
        value_rows = jnp.concatenate([value[cut], ones], axis=0).astype(BF16)
        up_rows = jnp.concatenate([up_wide, rows_in], axis=0).astype(BF16)
        centred = dot(value_rows, up_rows, ((0,), (0,)))
        score_grad = (weights.astype(F32) * centred).astype(BF16)
        query_grad = dot(key_nrm, score_grad, ((1,), (0,))) * factor
        key_grad = dot(query_nrm, score_grad, ((1,), (1,))) * factor
        value_grad = dot(up, weights, ((1,), (1,)))
        grads.append(
            (
                norm_back(query_grad, query_hat, query_inv, query_gain),
                norm_back(key_grad, key_hat, key_inv, key_gain),
                value_grad,
            )
        )
    for n in range(3):
        whole = jnp.concatenate([grad[n] for grad in grads], axis=0).astype(BF16)
        for s in range(count):
            out_refs[s][n] = whole[:, s * LANES : (s + 1) * LANES]


def space_bwd(axis, parts, gains, weights, attended, up, arrays):
    count = len(arrays)
    _, rows, tokens = arrays[0].shape
    return pl.pallas_call(
        functools.partial(space_bwd_kernel, axis, parts),
        out_shape=[jax.ShapeDtypeStruct((3, rows, tokens), BF16)] * count,
        scratch_shapes=[pltpu.VMEM((rows, count * tokens), F32)],
        compiler_params=PARAMS,
        cost_estimate=cost(6),
        name="space_bwd",
    )(gains, weights, attended, up, *arrays)


def time_head(query_in, key_in, value, upward, query_gain, key_gain, parts):
    width = LANES // parts
    factor = HD ** (-0.5)
    query_hat, query_inv = head_norm(query_in)
    key_hat, key_inv = head_norm(key_in)
    query_nrm = rounded(query_hat * query_gain)
    key_nrm = rounded(key_hat * key_gain)

    def turned(tensor, r):
        shift = (r * width) % LANES
        return tensor if shift == 0 else pltpu.roll(tensor, shift, 1)

    keys = [turned(key_nrm, r) for r in range(parts)]
    expons = [jnp.exp(jnp.sum(query_nrm * keys[r], axis=0, keepdims=True) * factor) for r in range(parts)]
    scale = 1.0 / functools.reduce(jnp.add, expons)
    shares = [expon * scale for expon in expons]
    share_grads = [jnp.sum(upward * turned(value, r), axis=0, keepdims=True) for r in range(parts)]
    centre = functools.reduce(jnp.add, [a * b for a, b in zip(shares, share_grads)])
    score_grads = [rounded(shares[r] * (share_grads[r] - centre) * factor) for r in range(parts)]
    query_grad = functools.reduce(jnp.add, [score_grads[r] * keys[r] for r in range(parts)])
    key_grad = functools.reduce(jnp.add, [turned(score_grads[r] * query_nrm, -r) for r in range(parts)])
    value_grad = functools.reduce(jnp.add, [turned(rounded(shares[r]) * upward, -r) for r in range(parts)])
    return (
        norm_back(query_grad, query_hat, query_inv, query_gain),
        norm_back(key_grad, key_hat, key_inv, key_gain),
        value_grad,
    )


def middle_kernel(
    frame_axis, count, parts, att_ref, pair_ref, gain_ref, ow_hbm, qw_hbm, up_ref, *refs
):
    gr_refs = refs[:parts]
    ow_ref, qw_ref, att_s, low_s, cot_s, qkv_s, grad_s, back_s, sems = refs[parts:]
    width = ow_ref.shape[0]
    rows = width // count
    copies = [pltpu.make_async_copy(ow_hbm, ow_ref, sems.at[3])]
    copies += [pltpu.make_async_copy(qw_hbm.at[n], qw_ref.at[n], sems.at[n]) for n in range(3)]
    for copy in copies:
        copy.start()
    for z in range(count):
        att_s[z * rows : (z + 1) * rows, :] = unpack(
            [att_ref[z * parts + f].astype(F32) for f in range(parts)]
        )
    attended = att_s[...].T.astype(BF16)
    cot_s[...] = pair_ref[:, 1].reshape(LANES, width).astype(F32).T
    copies[0].wait()
    mixed = rounded(
        pair_ref[:, 0].reshape(LANES, width).astype(F32) + dot(attended, ow_ref[...], ((1,), (0,)))
    )
    centred = mixed - jnp.mean(mixed, axis=1, keepdims=True)
    inverse = lax.rsqrt(jnp.mean(centred * centred, axis=1, keepdims=True) + EPS)
    normed = centred * inverse
    low_s[...] = normed
    lowered = normed.astype(BF16)
    for n in range(3):
        copies[1 + n].wait()
        product = rounded(dot(lowered, qw_ref[n], ((1,), (0,))))
        qkv_s[n] = product.T
    query_gain, key_gain = (column(gain_ref[n : n + 1]) for n in range(2))
    for h in range(width // HD):
        cut = slice(h * HD, (h + 1) * HD)
        grads = time_head(
            qkv_s[0, cut], qkv_s[1, cut], qkv_s[2, cut], cot_s[cut], query_gain, key_gain, parts
        )
        for n in range(3):
            grad_s[n, cut] = grads[n]
    upward = dot(qw_ref[0], grad_s[0].astype(BF16), ((1,), (0,)))
    upward = upward + dot(qw_ref[1], grad_s[1].astype(BF16), ((1,), (0,)))
    upward = upward + dot(qw_ref[2], grad_s[2].astype(BF16), ((1,), (0,)))
    upward = upward.T
    grad = inverse * (
        upward
        - jnp.mean(upward, axis=1, keepdims=True)
        - low_s[...] * jnp.mean(upward * low_s[...], axis=1, keepdims=True)
    )
    grad = grad.astype(BF16)
    back_s[...] = grad.reshape(back_s.shape)
    mine = lax.axis_index(frame_axis)
    for s, ref in enumerate(gr_refs):
        ref[...] = back_s[mine ^ s]
    att_s[...] = dot(ow_ref[...], grad, ((1,), (1,)))
    for z in range(count):
        for f, block in enumerate(pack(att_s[z * rows : (z + 1) * rows, :], parts)):
            up_ref[z * parts + f] = block.astype(BF16)


def middle(frame_axis, count, parts, att, pair, gains, out_weight, qkv_weight):
    width = out_weight.shape[0]
    vmem = pl.BlockSpec(memory_space=pltpu.VMEM)
    outs = pl.pallas_call(
        functools.partial(middle_kernel, frame_axis, count, parts),
        out_shape=[jax.ShapeDtypeStruct(att.shape, BF16)]
        + [jax.ShapeDtypeStruct(pair.shape[2:], BF16)] * parts,
        in_specs=[vmem] * 3 + [pl.BlockSpec(memory_space=pltpu.HBM)] * 2,
        scratch_shapes=[
            pltpu.VMEM(out_weight.shape, BF16),
            pltpu.VMEM(qkv_weight.shape, BF16),
            pltpu.VMEM((width, LANES), F32),
            pltpu.VMEM((LANES, width), F32),
            pltpu.VMEM((width, LANES), F32),
            pltpu.VMEM((3, width, LANES), F32),
            pltpu.VMEM((3, width, LANES), F32),
            pltpu.VMEM((parts,) + pair.shape[2:], BF16),
            pltpu.SemaphoreType.DMA((4,)),
        ],
        compiler_params=PARAMS,
        cost_estimate=cost(10),
        name="middle",
    )(att, pair, gains, in_hbm(out_weight), in_hbm(qkv_weight))
    return outs[0], outs[1:]


def swap(array, axis, count, s):
    if s == 0:
        return array
    return lax.ppermute(array, axis, [(n, n ^ s) for n in range(count)])


def local(
    count,
    parts,
    residual,
    spatial_query,
    spatial_key,
    spatial_value,
    out_weight,
    qkv_weight,
    space_gains,
    time_gains,
    cotangent,
):
    tokens, width = residual.shape[1:]
    both, own = turn(
        "seq",
        count,
        parts,
        (spatial_query[0], spatial_key[0], spatial_value[0]),
        (residual[0], cotangent[0]),
    )
    held = [swap(own[s], "seq", count, s) for s in range(count)]
    both = lax.all_to_all(both, "frm", 0, 0, tiled=True)
    sent = space_fwd("seq", parts, space_gains, held)
    att = lax.all_to_all(sent, ("seq", "frm"), 0, 0, tiled=True)
    late = lax.optimization_barrier((sent, *held))[1:]
    weights, attended = space_weights(space_gains, late)
    att, both, weights, attended = lax.optimization_barrier((att, both, weights, attended))
    up, grad = middle("frm", count, parts, att, both, time_gains, out_weight, qkv_weight)
    up = lax.all_to_all(up, ("seq", "frm"), 0, 0, tiled=True)
    grads = space_bwd("seq", parts, space_gains, weights, attended, up, held)
    back = [swap(grads[s], "seq", count, s) for s in range(count)]
    grad = lax.optimization_barrier((*grad, back[1]))[:-1]
    grad = [swap(grad[s], "frm", parts, s) for s in range(parts)]
    grad_query, grad_key, grad_value, grad = unturn("seq", "frm", back, grad)
    return (
        grad.reshape((1, tokens, width)),
        grad_query[None],
        grad_key[None],
        grad_value[None],
    )


def solution(mesh):
    tokens = P(("grp", "frm"), "seq", None)
    return jax.shard_map(
        functools.partial(local, mesh.shape["seq"], mesh.shape["frm"]),
        mesh=mesh,
        in_specs=(tokens, tokens, tokens, tokens, P(), P(), P(), P(), tokens),
        out_specs=(tokens, tokens, tokens, tokens),
        check_vma=False,
    )
```

```python
import functools

import jax
import jax.numpy as jnp
from jax import lax
from jax.experimental import pallas as pl
from jax.experimental.pallas import tpu as pltpu
from jax.sharding import PartitionSpec as P

HD = 72
EPS = 1e-06
F32 = jnp.float32
BF16 = jnp.bfloat16
LANES = 128
VMEM_LIMIT = 40 * 1024 * 1024

PARAMS = pltpu.CompilerParams(vmem_limit_bytes=VMEM_LIMIT)


def in_hbm(array):
    return pltpu.with_memory_space_constraint(array, pltpu.HBM)


def cost(micros):
    return pl.CostEstimate(flops=int(micros * 1e9), bytes_accessed=0, transcendentals=0)


def dot(left, right, dims):
    return lax.dot_general(left, right, (dims, ((), ())), preferred_element_type=F32)


def rounded(value):
    return value.astype(BF16).astype(F32)


def head_norm(tensor):
    inverse = lax.rsqrt(jnp.mean(tensor * tensor, axis=-2, keepdims=True) + EPS)
    return (tensor * inverse, inverse)


def norm_back(upward, hat, inverse, gain):
    scaled = upward * gain
    return inverse * (scaled - hat * jnp.mean(scaled * hat, axis=-2, keepdims=True))


def exchange_lanes(blocks, width):
    count = len(blocks)
    group = lax.broadcasted_iota(jnp.int32, blocks[0].shape, 1) // width
    results = []
    for a in range(count):
        result = None
        for b in range(count):
            shift = (width * (b - a)) % (width * count)
            moved = blocks[b] if shift == 0 else pltpu.roll(blocks[b], shift, 1)
            result = moved if result is None else jnp.where(group == b, moved, result)
        results.append(result)
    return results


def column(row):
    size = row.shape[1]
    here = lax.broadcasted_iota(jnp.int32, (size, size), 0) == lax.broadcasted_iota(
        jnp.int32, (size, size), 1
    )
    return jnp.sum(jnp.where(here, row, 0.0), axis=1, keepdims=True)


def is_dense(rows, parts):
    return rows % (8 * parts) == 0


def pack(tile, parts):
    rows, width = tile.shape[0], tile.shape[1] // parts
    if is_dense(rows, parts):
        own = rows // parts
        return exchange_lanes([tile[b * own : (b + 1) * own] for b in range(parts)], width)
    return [tile[:, b * width : (b + 1) * width] for b in range(parts)]


def unpack(blocks):
    parts = len(blocks)
    if blocks[0].shape[1] * parts == LANES:
        return jnp.concatenate(blocks, axis=1)
    return jnp.concatenate(exchange_lanes(blocks, blocks[0].shape[1] // parts), axis=0)


def block_shape(rows, parts):
    if is_dense(rows, parts):
        return (rows // parts, LANES)
    return (rows, LANES // parts)


def turn_kernel(axis, *refs):
    in_refs, out_refs = refs[:3], refs[3:-3]
    landed, held, sems = refs[-3:]
    rows = out_refs[0].shape[1]
    me = lax.axis_index(axis)
    copies = [pltpu.make_async_copy(ref, landed.at[n], sems.at[n]) for n, ref in enumerate(in_refs)]
    for copy in copies:
        copy.start()
    for n, copy in enumerate(copies):
        copy.wait()
        held[n] = landed[n].T
    for s, ref in enumerate(out_refs):
        start = pl.multiple_of((me ^ s) * rows, rows)
        ref[...] = held[:, pl.ds(start, rows), :]


def turn(axis, count, arrays):
    tokens, width = arrays[0].shape
    return pl.pallas_call(
        functools.partial(turn_kernel, axis),
        out_shape=[jax.ShapeDtypeStruct((3, width // count, tokens), BF16)] * count,
        in_specs=[pl.BlockSpec(memory_space=pltpu.HBM)] * 3,
        scratch_shapes=[
            pltpu.VMEM((3, tokens, width), BF16),
            pltpu.VMEM((3, width, tokens), BF16),
            pltpu.SemaphoreType.DMA((3,)),
        ],
        compiler_params=PARAMS,
        cost_estimate=cost(3),
        name="turn",
    )(*(in_hbm(array) for array in arrays))


def frames_kernel(res_hbm, cot_hbm, both_ref, landed, sems):
    parts, _, own, width = both_ref.shape
    copies = [
        pltpu.make_async_copy(ref, landed.at[n], sems.at[n]) for n, ref in enumerate((res_hbm, cot_hbm))
    ]
    for copy in copies:
        copy.start()
    for n, copy in enumerate(copies):
        copy.wait()
        both_ref[:, n] = landed[n].reshape(parts, own, width)


def frames(parts, residual, cotangent):
    tokens, width = residual.shape
    return pl.pallas_call(
        frames_kernel,
        out_shape=jax.ShapeDtypeStruct((parts, 2, tokens // parts, width), BF16),
        in_specs=[pl.BlockSpec(memory_space=pltpu.HBM)] * 2,
        scratch_shapes=[
            pltpu.VMEM((2, tokens, width), BF16),
            pltpu.SemaphoreType.DMA((2,)),
        ],
        compiler_params=PARAMS,
        cost_estimate=cost(2),
        name="frames",
    )(in_hbm(residual), in_hbm(cotangent))


def unturn_kernel(axis, frame_axis, count, *refs):
    in_refs, frame_refs = refs[:count], refs[count:-5]
    out_refs, grad_out, held = refs[-5:-2], refs[-2], refs[-1]
    rows = in_refs[0].shape[1]
    me, mine = lax.axis_index(axis), lax.axis_index(frame_axis)
    for s, ref in enumerate(frame_refs):
        grad_out[mine ^ s] = ref[...]
    for s, ref in enumerate(in_refs):
        start = pl.multiple_of((me ^ s) * rows, rows)
        held[:, pl.ds(start, rows), :] = ref[...]
    for n, ref in enumerate(out_refs):
        ref[...] = held[n].T


def unturn(axis, frame_axis, blocks, frame_blocks):
    count = len(blocks)
    _, rows, tokens = blocks[0].shape
    return pl.pallas_call(
        functools.partial(unturn_kernel, axis, frame_axis, count),
        out_shape=[jax.ShapeDtypeStruct((tokens, rows * count), BF16)] * 3
        + [jax.ShapeDtypeStruct((len(frame_blocks),) + frame_blocks[0].shape, BF16)],
        scratch_shapes=[pltpu.VMEM((3, rows * count, tokens), BF16)],
        compiler_params=PARAMS,
        cost_estimate=cost(3),
        name="unturn",
    )(*blocks, *frame_blocks)


def gather_part(refs, part):
    return jnp.concatenate([ref[part].astype(F32) for ref in refs], axis=1)


def head_expons(query, key, query_gain, key_gain):
    query_nrm = (head_norm(query)[0] * query_gain).astype(BF16)
    key_nrm = (head_norm(key)[0] * key_gain).astype(BF16)
    expons = jnp.exp(dot(key_nrm, query_nrm, ((0,), (0,))) * (HD ** (-0.5)))
    return expons, 1.0 / jnp.sum(expons, axis=0, keepdims=True)


def space_fwd_kernel(axis, parts, gain_ref, *refs):
    in_refs, out_ref, held = refs[:-2], refs[-2], refs[-1]
    count = len(in_refs)
    rows = in_refs[0].shape[1]
    me = lax.axis_index(axis)
    query, key, value = (gather_part(in_refs, n) for n in range(3))
    query_gain, key_gain = (column(gain_ref[n : n + 1]) for n in range(2))
    for h in range(rows // HD):
        cut = slice(h * HD, (h + 1) * HD)
        expons, scale = head_expons(query[cut], key[cut], query_gain, key_gain)
        attended = dot(value[cut].astype(BF16), expons.astype(BF16), ((1,), (0,)))
        held[cut, :] = attended * scale
    for s in range(count):
        blocks = pack(held[:, s * LANES : (s + 1) * LANES], parts)
        for f, block in enumerate(blocks):
            out_ref[(me ^ s) * parts + f] = block.astype(BF16)


def space_fwd(axis, parts, gains, arrays):
    count = len(arrays)
    _, rows, tokens = arrays[0].shape
    return pl.pallas_call(
        functools.partial(space_fwd_kernel, axis, parts),
        out_shape=jax.ShapeDtypeStruct((count * parts,) + block_shape(rows, parts), BF16),
        scratch_shapes=[pltpu.VMEM((rows, count * tokens), F32)],
        compiler_params=PARAMS,
        cost_estimate=cost(4),
        name="space_fwd",
    )(gains, *arrays)


def space_weights_kernel(gain_ref, *refs):
    in_refs, weight_ref, att_ref = refs[:-2], refs[-2], refs[-1]
    query, key, value = (gather_part(in_refs, n) for n in range(3))
    query_gain, key_gain = (column(gain_ref[n : n + 1]) for n in range(2))
    for h in range(weight_ref.shape[0]):
        cut = slice(h * HD, (h + 1) * HD)
        expons, scale = head_expons(query[cut], key[cut], query_gain, key_gain)
        weights = (expons * scale).astype(BF16)
        weight_ref[h] = weights
        att_ref[cut, :] = dot(value[cut].astype(BF16), weights, ((1,), (0,)))


def space_weights(gains, arrays):
    count = len(arrays)
    _, rows, tokens = arrays[0].shape
    return pl.pallas_call(
        space_weights_kernel,
        out_shape=[
            jax.ShapeDtypeStruct((rows // HD, count * tokens, count * tokens), BF16),
            jax.ShapeDtypeStruct((rows, count * tokens), F32),
        ],
        compiler_params=PARAMS,
        cost_estimate=cost(8),
        name="space_weights",
    )(gains, *arrays)


def space_bwd_kernel(axis, parts, gain_ref, weight_ref, att_ref, up_ref, *refs):
    count = (len(refs) - 1) // 2
    in_refs, out_refs, held = refs[:count], refs[count:-1], refs[-1]
    rows = in_refs[0].shape[1]
    me = lax.axis_index(axis)
    for s in range(count):
        blocks = [up_ref[(me ^ s) * parts + f].astype(F32) for f in range(parts)]
        held[:, s * LANES : (s + 1) * LANES] = unpack(blocks)
    query, key, value = (gather_part(in_refs, n) for n in range(3))
    query_gain, key_gain = (column(gain_ref[n : n + 1]) for n in range(2))
    factor = HD ** (-0.5)
    extra = lax.broadcasted_iota(jnp.int32, (8, query.shape[1]), 0)
    ones = jnp.where(extra < 2, 1.0, 0.0)
    grads = []
    for h in range(rows // HD):
        cut = slice(h * HD, (h + 1) * HD)
        query_hat, query_inv = head_norm(query[cut])
        key_hat, key_inv = head_norm(key[cut])
        query_nrm = (query_hat * query_gain).astype(BF16)
        key_nrm = (key_hat * key_gain).astype(BF16)
        up_wide = held[cut, :]
        up = up_wide.astype(BF16)
        weights = weight_ref[h]
        centre = jnp.sum(up_wide * att_ref[cut, :], axis=0, keepdims=True)
        high = rounded(centre)
        rows_in = jnp.where(extra == 0, -high, jnp.where(extra == 1, high - centre, 0.0))
        value_rows = jnp.concatenate([value[cut], ones], axis=0).astype(BF16)
        up_rows = jnp.concatenate([up_wide, rows_in], axis=0).astype(BF16)
        centred = dot(value_rows, up_rows, ((0,), (0,)))
        score_grad = (weights.astype(F32) * centred).astype(BF16)
        query_grad = dot(key_nrm, score_grad, ((1,), (0,))) * factor
        key_grad = dot(query_nrm, score_grad, ((1,), (1,))) * factor
        value_grad = dot(up, weights, ((1,), (1,)))
        grads.append(
            (
                norm_back(query_grad, query_hat, query_inv, query_gain),
                norm_back(key_grad, key_hat, key_inv, key_gain),
                value_grad,
            )
        )
    for n in range(3):
        whole = jnp.concatenate([grad[n] for grad in grads], axis=0).astype(BF16)
        for s in range(count):
            out_refs[s][n] = whole[:, s * LANES : (s + 1) * LANES]


def space_bwd(axis, parts, gains, weights, attended, up, arrays):
    count = len(arrays)
    _, rows, tokens = arrays[0].shape
    return pl.pallas_call(
        functools.partial(space_bwd_kernel, axis, parts),
        out_shape=[jax.ShapeDtypeStruct((3, rows, tokens), BF16)] * count,
        scratch_shapes=[pltpu.VMEM((rows, count * tokens), F32)],
        compiler_params=PARAMS,
        cost_estimate=cost(6),
        name="space_bwd",
    )(gains, weights, attended, up, *arrays)


def time_head(query_in, key_in, value, upward, query_gain, key_gain, parts):
    width = LANES // parts
    factor = HD ** (-0.5)
    query_hat, query_inv = head_norm(query_in)
    key_hat, key_inv = head_norm(key_in)
    query_nrm = rounded(query_hat * query_gain)
    key_nrm = rounded(key_hat * key_gain)

    def turned(tensor, r):
        shift = (r * width) % LANES
        return tensor if shift == 0 else pltpu.roll(tensor, shift, 1)

    keys = [turned(key_nrm, r) for r in range(parts)]
    expons = [jnp.exp(jnp.sum(query_nrm * keys[r], axis=0, keepdims=True) * factor) for r in range(parts)]
    scale = 1.0 / functools.reduce(jnp.add, expons)
    shares = [expon * scale for expon in expons]
    share_grads = [jnp.sum(upward * turned(value, r), axis=0, keepdims=True) for r in range(parts)]
    centre = functools.reduce(jnp.add, [a * b for a, b in zip(shares, share_grads)])
    score_grads = [rounded(shares[r] * (share_grads[r] - centre) * factor) for r in range(parts)]
    query_grad = functools.reduce(jnp.add, [score_grads[r] * keys[r] for r in range(parts)])
    key_grad = functools.reduce(jnp.add, [turned(score_grads[r] * query_nrm, -r) for r in range(parts)])
    value_grad = functools.reduce(jnp.add, [turned(rounded(shares[r]) * upward, -r) for r in range(parts)])
    return (
        norm_back(query_grad, query_hat, query_inv, query_gain),
        norm_back(key_grad, key_hat, key_inv, key_gain),
        value_grad,
    )


def middle_kernel(
    frame_axis, count, parts, att_ref, pair_ref, gain_ref, ow_hbm, qw_hbm, up_ref, *refs
):
    gr_refs = refs[:parts]
    ow_ref, qw_ref, att_s, low_s, cot_s, qkv_s, grad_s, back_s, sems = refs[parts:]
    width = ow_ref.shape[0]
    rows = width // count
    copies = [pltpu.make_async_copy(ow_hbm, ow_ref, sems.at[3])]
    copies += [pltpu.make_async_copy(qw_hbm.at[n], qw_ref.at[n], sems.at[n]) for n in range(3)]
    for copy in copies:
        copy.start()
    for z in range(count):
        att_s[z * rows : (z + 1) * rows, :] = unpack(
            [att_ref[z * parts + f].astype(F32) for f in range(parts)]
        )
    attended = att_s[...].T.astype(BF16)
    cot_s[...] = pair_ref[:, 1].reshape(LANES, width).astype(F32).T
    copies[0].wait()
    mixed = rounded(
        pair_ref[:, 0].reshape(LANES, width).astype(F32) + dot(attended, ow_ref[...], ((1,), (0,)))
    )
    centred = mixed - jnp.mean(mixed, axis=1, keepdims=True)
    inverse = lax.rsqrt(jnp.mean(centred * centred, axis=1, keepdims=True) + EPS)
    normed = centred * inverse
    low_s[...] = normed
    lowered = normed.astype(BF16)
    for n in range(3):
        copies[1 + n].wait()
        product = rounded(dot(lowered, qw_ref[n], ((1,), (0,))))
        qkv_s[n] = product.T
    query_gain, key_gain = (column(gain_ref[n : n + 1]) for n in range(2))
    for h in range(width // HD):
        cut = slice(h * HD, (h + 1) * HD)
        grads = time_head(
            qkv_s[0, cut], qkv_s[1, cut], qkv_s[2, cut], cot_s[cut], query_gain, key_gain, parts
        )
        for n in range(3):
            grad_s[n, cut] = grads[n]
    upward = dot(qw_ref[0], grad_s[0].astype(BF16), ((1,), (0,)))
    upward = upward + dot(qw_ref[1], grad_s[1].astype(BF16), ((1,), (0,)))
    upward = upward + dot(qw_ref[2], grad_s[2].astype(BF16), ((1,), (0,)))
    upward = upward.T
    grad = inverse * (
        upward
        - jnp.mean(upward, axis=1, keepdims=True)
        - low_s[...] * jnp.mean(upward * low_s[...], axis=1, keepdims=True)
    )
    grad = grad.astype(BF16)
    back_s[...] = grad.reshape(back_s.shape)
    mine = lax.axis_index(frame_axis)
    for s, ref in enumerate(gr_refs):
        ref[...] = back_s[mine ^ s]
    att_s[...] = dot(ow_ref[...], grad, ((1,), (1,)))
    for z in range(count):
        for f, block in enumerate(pack(att_s[z * rows : (z + 1) * rows, :], parts)):
            up_ref[z * parts + f] = block.astype(BF16)


def middle(frame_axis, count, parts, att, pair, gains, out_weight, qkv_weight):
    width = out_weight.shape[0]
    vmem = pl.BlockSpec(memory_space=pltpu.VMEM)
    outs = pl.pallas_call(
        functools.partial(middle_kernel, frame_axis, count, parts),
        out_shape=[jax.ShapeDtypeStruct(att.shape, BF16)]
        + [jax.ShapeDtypeStruct(pair.shape[2:], BF16)] * parts,
        in_specs=[vmem] * 3 + [pl.BlockSpec(memory_space=pltpu.HBM)] * 2,
        scratch_shapes=[
            pltpu.VMEM(out_weight.shape, BF16),
            pltpu.VMEM(qkv_weight.shape, BF16),
            pltpu.VMEM((width, LANES), F32),
            pltpu.VMEM((LANES, width), F32),
            pltpu.VMEM((width, LANES), F32),
            pltpu.VMEM((3, width, LANES), F32),
            pltpu.VMEM((3, width, LANES), F32),
            pltpu.VMEM((parts,) + pair.shape[2:], BF16),
            pltpu.SemaphoreType.DMA((4,)),
        ],
        compiler_params=PARAMS,
        cost_estimate=cost(10),
        name="middle",
    )(att, pair, gains, in_hbm(out_weight), in_hbm(qkv_weight))
    return outs[0], outs[1:]


def swap(array, axis, count, s):
    if s == 0:
        return array
    return lax.ppermute(array, axis, [(n, n ^ s) for n in range(count)])


def local(
    count,
    parts,
    residual,
    spatial_query,
    spatial_key,
    spatial_value,
    out_weight,
    qkv_weight,
    space_gains,
    time_gains,
    cotangent,
):
    tokens, width = residual.shape[1:]
    own = turn("seq", count, (spatial_query[0], spatial_key[0], spatial_value[0]))
    residual, cotangent, _ = lax.optimization_barrier((residual, cotangent, own[0]))
    both = frames(parts, residual[0], cotangent[0])
    held = [swap(own[s], "seq", count, s) for s in range(count)]
    both = lax.all_to_all(both, "frm", 0, 0, tiled=True)
    sent = space_fwd("seq", parts, space_gains, held)
    att = lax.all_to_all(sent, ("seq", "frm"), 0, 0, tiled=True)
    late = lax.optimization_barrier((sent, *held))[1:]
    weights, attended = space_weights(space_gains, late)
    att, both, weights, attended = lax.optimization_barrier((att, both, weights, attended))
    up, grad = middle("frm", count, parts, att, both, time_gains, out_weight, qkv_weight)
    up = lax.all_to_all(up, ("seq", "frm"), 0, 0, tiled=True)
    grads = space_bwd("seq", parts, space_gains, weights, attended, up, held)
    back = [swap(grads[s], "seq", count, s) for s in range(count)]
    grad = lax.optimization_barrier((*grad, back[1]))[:-1]
    grad = [swap(grad[s], "frm", parts, s) for s in range(parts)]
    grad_query, grad_key, grad_value, grad = unturn("seq", "frm", back, grad)
    return (
        grad.reshape((1, tokens, width)),
        grad_query[None],
        grad_key[None],
        grad_value[None],
    )


def solution(mesh):
    tokens = P(("grp", "frm"), "seq", None)
    return jax.shard_map(
        functools.partial(local, mesh.shape["seq"], mesh.shape["frm"]),
        mesh=mesh,
        in_specs=(tokens, tokens, tokens, tokens, P(), P(), P(), P(), tokens),
        out_specs=(tokens, tokens, tokens, tokens),
        check_vma=False,
    )
```

```python
import functools

import jax
import jax.numpy as jnp
from jax import lax
from jax.experimental import pallas as pl
from jax.experimental.pallas import tpu as pltpu
from jax.sharding import PartitionSpec as P

HD = 72
EPS = 1e-06
F32 = jnp.float32
BF16 = jnp.bfloat16
LANES = 128
VMEM_LIMIT = 40 * 1024 * 1024

PARAMS = pltpu.CompilerParams(vmem_limit_bytes=VMEM_LIMIT)


def in_hbm(array):
    return pltpu.with_memory_space_constraint(array, pltpu.HBM)


def cost(micros):
    return pl.CostEstimate(flops=int(micros * 1e9), bytes_accessed=0, transcendentals=0)


def dot(left, right, dims):
    return lax.dot_general(left, right, (dims, ((), ())), preferred_element_type=F32)


def rounded(value):
    return value.astype(BF16).astype(F32)


def head_norm(tensor):
    inverse = lax.rsqrt(jnp.mean(tensor * tensor, axis=-2, keepdims=True) + EPS)
    return (tensor * inverse, inverse)


def norm_back(upward, hat, inverse, gain):
    scaled = upward * gain
    return inverse * (scaled - hat * jnp.mean(scaled * hat, axis=-2, keepdims=True))


def exchange_lanes(blocks, width):
    count = len(blocks)
    group = lax.broadcasted_iota(jnp.int32, blocks[0].shape, 1) // width
    results = []
    for a in range(count):
        result = None
        for b in range(count):
            shift = (width * (b - a)) % (width * count)
            moved = blocks[b] if shift == 0 else pltpu.roll(blocks[b], shift, 1)
            result = moved if result is None else jnp.where(group == b, moved, result)
        results.append(result)
    return results


def column(row):
    size = row.shape[1]
    here = lax.broadcasted_iota(jnp.int32, (size, size), 0) == lax.broadcasted_iota(
        jnp.int32, (size, size), 1
    )
    return jnp.sum(jnp.where(here, row, 0.0), axis=1, keepdims=True)


def is_dense(rows, parts):
    return rows % (8 * parts) == 0


def pack(tile, parts):
    rows, width = tile.shape[0], tile.shape[1] // parts
    if is_dense(rows, parts):
        own = rows // parts
        return exchange_lanes([tile[b * own : (b + 1) * own] for b in range(parts)], width)
    return [tile[:, b * width : (b + 1) * width] for b in range(parts)]


def unpack(blocks):
    parts = len(blocks)
    if blocks[0].shape[1] * parts == LANES:
        return jnp.concatenate(blocks, axis=1)
    return jnp.concatenate(exchange_lanes(blocks, blocks[0].shape[1] // parts), axis=0)


def block_shape(rows, parts):
    if is_dense(rows, parts):
        return (rows // parts, LANES)
    return (rows, LANES // parts)


def turn_kernel(axis, *refs):
    in_refs, out_refs = refs[:3], refs[3:-3]
    landed, held, sems = refs[-3:]
    rows = out_refs[0].shape[1]
    me = lax.axis_index(axis)
    copies = [pltpu.make_async_copy(ref, landed.at[n], sems.at[n]) for n, ref in enumerate(in_refs)]
    for copy in copies:
        copy.start()
    for n, copy in enumerate(copies):
        copy.wait()
        held[n] = landed[n].T
    for s, ref in enumerate(out_refs):
        start = pl.multiple_of((me ^ s) * rows, rows)
        ref[...] = held[:, pl.ds(start, rows), :]


def turn(axis, count, arrays):
    tokens, width = arrays[0].shape
    return pl.pallas_call(
        functools.partial(turn_kernel, axis),
        out_shape=[jax.ShapeDtypeStruct((3, width // count, tokens), BF16)] * count,
        in_specs=[pl.BlockSpec(memory_space=pltpu.HBM)] * 3,
        scratch_shapes=[
            pltpu.VMEM((3, tokens, width), BF16),
            pltpu.VMEM((3, width, tokens), BF16),
            pltpu.SemaphoreType.DMA((3,)),
        ],
        compiler_params=PARAMS,
        cost_estimate=cost(3),
        name="turn",
    )(*(in_hbm(array) for array in arrays))


def frames_kernel(res_hbm, cot_hbm, both_ref, landed, sems):
    parts, _, own, width = both_ref.shape
    copies = [
        pltpu.make_async_copy(ref, landed.at[n], sems.at[n]) for n, ref in enumerate((res_hbm, cot_hbm))
    ]
    for copy in copies:
        copy.start()
    for n, copy in enumerate(copies):
        copy.wait()
        both_ref[:, n] = landed[n].reshape(parts, own, width)


def frames(parts, residual, cotangent):
    tokens, width = residual.shape
    return pl.pallas_call(
        frames_kernel,
        out_shape=jax.ShapeDtypeStruct((parts, 2, tokens // parts, width), BF16),
        in_specs=[pl.BlockSpec(memory_space=pltpu.HBM)] * 2,
        scratch_shapes=[
            pltpu.VMEM((2, tokens, width), BF16),
            pltpu.SemaphoreType.DMA((2,)),
        ],
        compiler_params=PARAMS,
        cost_estimate=cost(2),
        name="frames",
    )(in_hbm(residual), in_hbm(cotangent))


def unturn_kernel(axis, frame_axis, count, *refs):
    in_refs, frame_refs = refs[:count], refs[count:-5]
    out_refs, grad_out, held = refs[-5:-2], refs[-2], refs[-1]
    rows = in_refs[0].shape[1]
    me, mine = lax.axis_index(axis), lax.axis_index(frame_axis)
    for s, ref in enumerate(frame_refs):
        grad_out[mine ^ s] = ref[...]
    for s, ref in enumerate(in_refs):
        start = pl.multiple_of((me ^ s) * rows, rows)
        held[:, pl.ds(start, rows), :] = ref[...]
    for n, ref in enumerate(out_refs):
        ref[...] = held[n].T


def unturn(axis, frame_axis, blocks, frame_blocks):
    count = len(blocks)
    _, rows, tokens = blocks[0].shape
    return pl.pallas_call(
        functools.partial(unturn_kernel, axis, frame_axis, count),
        out_shape=[jax.ShapeDtypeStruct((tokens, rows * count), BF16)] * 3
        + [jax.ShapeDtypeStruct((len(frame_blocks),) + frame_blocks[0].shape, BF16)],
        scratch_shapes=[pltpu.VMEM((3, rows * count, tokens), BF16)],
        compiler_params=PARAMS,
        cost_estimate=cost(3),
        name="unturn",
    )(*blocks, *frame_blocks)


def gather_part(refs, part):
    return jnp.concatenate([ref[part].astype(F32) for ref in refs], axis=1)


def head_expons(query, key, query_gain, key_gain):
    query_nrm = (head_norm(query)[0] * query_gain).astype(BF16)
    key_nrm = (head_norm(key)[0] * key_gain).astype(BF16)
    return jnp.exp(dot(key_nrm, query_nrm, ((0,), (0,))) * (HD ** (-0.5)))


def space_fwd_kernel(axis, parts, gain_ref, *refs):
    in_refs, out_ref, held = refs[:-2], refs[-2], refs[-1]
    count = len(in_refs)
    rows = in_refs[0].shape[1]
    me = lax.axis_index(axis)
    query, key, value = (gather_part(in_refs, n) for n in range(3))
    query_gain, key_gain = (column(gain_ref[n : n + 1]) for n in range(2))
    ones = jnp.ones((8, query.shape[1]), F32)
    for h in range(rows // HD):
        cut = slice(h * HD, (h + 1) * HD)
        expons = head_expons(query[cut], key[cut], query_gain, key_gain)
        rows_in = jnp.concatenate([value[cut], ones], axis=0).astype(BF16)
        attended = dot(rows_in, expons.astype(BF16), ((1,), (0,)))
        held[cut, :] = attended[:HD] * (1.0 / attended[HD : HD + 1])
    for s in range(count):
        blocks = pack(held[:, s * LANES : (s + 1) * LANES], parts)
        for f, block in enumerate(blocks):
            out_ref[(me ^ s) * parts + f] = block.astype(BF16)


def space_fwd(axis, parts, gains, arrays):
    count = len(arrays)
    _, rows, tokens = arrays[0].shape
    return pl.pallas_call(
        functools.partial(space_fwd_kernel, axis, parts),
        out_shape=jax.ShapeDtypeStruct((count * parts,) + block_shape(rows, parts), BF16),
        scratch_shapes=[pltpu.VMEM((rows, count * tokens), F32)],
        compiler_params=PARAMS,
        cost_estimate=cost(4),
        name="space_fwd",
    )(gains, *arrays)


def space_weights_kernel(gain_ref, *refs):
    in_refs, weight_ref, att_ref = refs[:-2], refs[-2], refs[-1]
    query, key, value = (gather_part(in_refs, n) for n in range(3))
    query_gain, key_gain = (column(gain_ref[n : n + 1]) for n in range(2))
    for h in range(weight_ref.shape[0]):
        cut = slice(h * HD, (h + 1) * HD)
        expons = head_expons(query[cut], key[cut], query_gain, key_gain)
        weights = (expons * (1.0 / jnp.sum(expons, axis=0, keepdims=True))).astype(BF16)
        weight_ref[h] = weights
        att_ref[cut, :] = dot(value[cut].astype(BF16), weights, ((1,), (0,)))


def space_weights(gains, arrays):
    count = len(arrays)
    _, rows, tokens = arrays[0].shape
    return pl.pallas_call(
        space_weights_kernel,
        out_shape=[
            jax.ShapeDtypeStruct((rows // HD, count * tokens, count * tokens), BF16),
            jax.ShapeDtypeStruct((rows, count * tokens), F32),
        ],
        compiler_params=PARAMS,
        cost_estimate=cost(8),
        name="space_weights",
    )(gains, *arrays)


def space_bwd_kernel(axis, parts, gain_ref, weight_ref, att_ref, up_ref, *refs):
    count = (len(refs) - 1) // 2
    in_refs, out_refs, held = refs[:count], refs[count:-1], refs[-1]
    rows = in_refs[0].shape[1]
    me = lax.axis_index(axis)
    for s in range(count):
        blocks = [up_ref[(me ^ s) * parts + f].astype(F32) for f in range(parts)]
        held[:, s * LANES : (s + 1) * LANES] = unpack(blocks)
    query, key, value = (gather_part(in_refs, n) for n in range(3))
    query_gain, key_gain = (column(gain_ref[n : n + 1]) for n in range(2))
    factor = HD ** (-0.5)
    extra = lax.broadcasted_iota(jnp.int32, (8, query.shape[1]), 0)
    ones = jnp.where(extra < 2, 1.0, 0.0)
    grads = []
    for h in range(rows // HD):
        cut = slice(h * HD, (h + 1) * HD)
        query_hat, query_inv = head_norm(query[cut])
        key_hat, key_inv = head_norm(key[cut])
        query_nrm = (query_hat * query_gain).astype(BF16)
        key_nrm = (key_hat * key_gain).astype(BF16)
        up_wide = held[cut, :]
        up = up_wide.astype(BF16)
        weights = weight_ref[h]
        centre = jnp.sum(up_wide * att_ref[cut, :], axis=0, keepdims=True)
        high = rounded(centre)
        rows_in = jnp.where(extra == 0, -high, jnp.where(extra == 1, high - centre, 0.0))
        value_rows = jnp.concatenate([value[cut], ones], axis=0).astype(BF16)
        up_rows = jnp.concatenate([up_wide, rows_in], axis=0).astype(BF16)
        centred = dot(value_rows, up_rows, ((0,), (0,)))
        score_grad = (weights.astype(F32) * centred).astype(BF16)
        query_grad = dot(key_nrm, score_grad, ((1,), (0,))) * factor
        key_grad = dot(query_nrm, score_grad, ((1,), (1,))) * factor
        value_grad = dot(up, weights, ((1,), (1,)))
        grads.append(
            (
                norm_back(query_grad, query_hat, query_inv, query_gain),
                norm_back(key_grad, key_hat, key_inv, key_gain),
                value_grad,
            )
        )
    for n in range(3):
        whole = jnp.concatenate([grad[n] for grad in grads], axis=0).astype(BF16)
        for s in range(count):
            out_refs[s][n] = whole[:, s * LANES : (s + 1) * LANES]


def space_bwd(axis, parts, gains, weights, attended, up, arrays):
    count = len(arrays)
    _, rows, tokens = arrays[0].shape
    return pl.pallas_call(
        functools.partial(space_bwd_kernel, axis, parts),
        out_shape=[jax.ShapeDtypeStruct((3, rows, tokens), BF16)] * count,
        scratch_shapes=[pltpu.VMEM((rows, count * tokens), F32)],
        compiler_params=PARAMS,
        cost_estimate=cost(6),
        name="space_bwd",
    )(gains, weights, attended, up, *arrays)


def time_head(query_in, key_in, value, upward, query_gain, key_gain, parts):
    width = LANES // parts
    factor = HD ** (-0.5)
    query_hat, query_inv = head_norm(query_in)
    key_hat, key_inv = head_norm(key_in)
    query_nrm = rounded(query_hat * query_gain)
    key_nrm = rounded(key_hat * key_gain)

    def turned(tensor, r):
        shift = (r * width) % LANES
        return tensor if shift == 0 else pltpu.roll(tensor, shift, 1)

    keys = [turned(key_nrm, r) for r in range(parts)]
    expons = [jnp.exp(jnp.sum(query_nrm * keys[r], axis=0, keepdims=True) * factor) for r in range(parts)]
    scale = 1.0 / functools.reduce(jnp.add, expons)
    shares = [expon * scale for expon in expons]
    share_grads = [jnp.sum(upward * turned(value, r), axis=0, keepdims=True) for r in range(parts)]
    centre = functools.reduce(jnp.add, [a * b for a, b in zip(shares, share_grads)])
    score_grads = [rounded(shares[r] * (share_grads[r] - centre) * factor) for r in range(parts)]
    query_grad = functools.reduce(jnp.add, [score_grads[r] * keys[r] for r in range(parts)])
    key_grad = functools.reduce(jnp.add, [turned(score_grads[r] * query_nrm, -r) for r in range(parts)])
    value_grad = functools.reduce(jnp.add, [turned(rounded(shares[r]) * upward, -r) for r in range(parts)])
    return (
        norm_back(query_grad, query_hat, query_inv, query_gain),
        norm_back(key_grad, key_hat, key_inv, key_gain),
        value_grad,
    )


def middle_kernel(
    frame_axis, count, parts, att_ref, pair_ref, gain_ref, ow_hbm, qw_hbm, up_ref, *refs
):
    gr_refs = refs[:parts]
    ow_ref, qw_ref, att_s, low_s, cot_s, qkv_s, grad_s, back_s, sems = refs[parts:]
    width = ow_ref.shape[0]
    rows = width // count
    copies = [pltpu.make_async_copy(ow_hbm, ow_ref, sems.at[3])]
    copies += [pltpu.make_async_copy(qw_hbm.at[n], qw_ref.at[n], sems.at[n]) for n in range(3)]
    for copy in copies:
        copy.start()
    for z in range(count):
        att_s[z * rows : (z + 1) * rows, :] = unpack(
            [att_ref[z * parts + f].astype(F32) for f in range(parts)]
        )
    attended = att_s[...].T.astype(BF16)
    cot_s[...] = pair_ref[:, 1].reshape(LANES, width).astype(F32).T
    copies[0].wait()
    mixed = rounded(
        pair_ref[:, 0].reshape(LANES, width).astype(F32) + dot(attended, ow_ref[...], ((1,), (0,)))
    )
    centred = mixed - jnp.mean(mixed, axis=1, keepdims=True)
    inverse = lax.rsqrt(jnp.mean(centred * centred, axis=1, keepdims=True) + EPS)
    normed = centred * inverse
    low_s[...] = normed
    lowered = normed.astype(BF16)
    for n in range(3):
        copies[1 + n].wait()
        product = rounded(dot(lowered, qw_ref[n], ((1,), (0,))))
        qkv_s[n] = product.T
    query_gain, key_gain = (column(gain_ref[n : n + 1]) for n in range(2))
    for h in range(width // HD):
        cut = slice(h * HD, (h + 1) * HD)
        grads = time_head(
            qkv_s[0, cut], qkv_s[1, cut], qkv_s[2, cut], cot_s[cut], query_gain, key_gain, parts
        )
        for n in range(3):
            grad_s[n, cut] = grads[n]
    upward = dot(qw_ref[0], grad_s[0].astype(BF16), ((1,), (0,)))
    upward = upward + dot(qw_ref[1], grad_s[1].astype(BF16), ((1,), (0,)))
    upward = upward + dot(qw_ref[2], grad_s[2].astype(BF16), ((1,), (0,)))
    upward = upward.T
    grad = inverse * (
        upward
        - jnp.mean(upward, axis=1, keepdims=True)
        - low_s[...] * jnp.mean(upward * low_s[...], axis=1, keepdims=True)
    )
    grad = grad.astype(BF16)
    back_s[...] = grad.reshape(back_s.shape)
    mine = lax.axis_index(frame_axis)
    for s, ref in enumerate(gr_refs):
        ref[...] = back_s[mine ^ s]
    att_s[...] = dot(ow_ref[...], grad, ((1,), (1,)))
    for z in range(count):
        for f, block in enumerate(pack(att_s[z * rows : (z + 1) * rows, :], parts)):
            up_ref[z * parts + f] = block.astype(BF16)


def middle(frame_axis, count, parts, att, pair, gains, out_weight, qkv_weight):
    width = out_weight.shape[0]
    vmem = pl.BlockSpec(memory_space=pltpu.VMEM)
    outs = pl.pallas_call(
        functools.partial(middle_kernel, frame_axis, count, parts),
        out_shape=[jax.ShapeDtypeStruct(att.shape, BF16)]
        + [jax.ShapeDtypeStruct(pair.shape[2:], BF16)] * parts,
        in_specs=[vmem] * 3 + [pl.BlockSpec(memory_space=pltpu.HBM)] * 2,
        scratch_shapes=[
            pltpu.VMEM(out_weight.shape, BF16),
            pltpu.VMEM(qkv_weight.shape, BF16),
            pltpu.VMEM((width, LANES), F32),
            pltpu.VMEM((LANES, width), F32),
            pltpu.VMEM((width, LANES), F32),
            pltpu.VMEM((3, width, LANES), F32),
            pltpu.VMEM((3, width, LANES), F32),
            pltpu.VMEM((parts,) + pair.shape[2:], BF16),
            pltpu.SemaphoreType.DMA((4,)),
        ],
        compiler_params=PARAMS,
        cost_estimate=cost(10),
        name="middle",
    )(att, pair, gains, in_hbm(out_weight), in_hbm(qkv_weight))
    return outs[0], outs[1:]


def swap(array, axis, count, s):
    if s == 0:
        return array
    return lax.ppermute(array, axis, [(n, n ^ s) for n in range(count)])


def local(
    count,
    parts,
    residual,
    spatial_query,
    spatial_key,
    spatial_value,
    out_weight,
    qkv_weight,
    space_gains,
    time_gains,
    cotangent,
):
    tokens, width = residual.shape[1:]
    own = turn("seq", count, (spatial_query[0], spatial_key[0], spatial_value[0]))
    residual, cotangent, _ = lax.optimization_barrier((residual, cotangent, own[0]))
    both = frames(parts, residual[0], cotangent[0])
    held = [swap(own[s], "seq", count, s) for s in range(count)]
    both = lax.all_to_all(both, "frm", 0, 0, tiled=True)
    sent = space_fwd("seq", parts, space_gains, held)
    att = lax.all_to_all(sent, ("seq", "frm"), 0, 0, tiled=True)
    late = lax.optimization_barrier((sent, *held))[1:]
    weights, attended = space_weights(space_gains, late)
    att, both, weights, attended = lax.optimization_barrier((att, both, weights, attended))
    up, grad = middle("frm", count, parts, att, both, time_gains, out_weight, qkv_weight)
    up = lax.all_to_all(up, ("seq", "frm"), 0, 0, tiled=True)
    grads = space_bwd("seq", parts, space_gains, weights, attended, up, held)
    back = [swap(grads[s], "seq", count, s) for s in range(count)]
    grad = lax.optimization_barrier((*grad, back[1]))[:-1]
    grad = [swap(grad[s], "frm", parts, s) for s in range(parts)]
    grad_query, grad_key, grad_value, grad = unturn("seq", "frm", back, grad)
    return (
        grad.reshape((1, tokens, width)),
        grad_query[None],
        grad_key[None],
        grad_value[None],
    )


def solution(mesh):
    tokens = P(("grp", "frm"), "seq", None)
    return jax.shard_map(
        functools.partial(local, mesh.shape["seq"], mesh.shape["frm"]),
        mesh=mesh,
        in_specs=(tokens, tokens, tokens, tokens, P(), P(), P(), P(), tokens),
        out_specs=(tokens, tokens, tokens, tokens),
        check_vma=False,
    )
```
